32 devices in a mesh: parts: 2 (over x), band: 8 (over z, y), depth: 2 (over core).
Axes of the slice: x: 2, y: 2, z: 4, core: 2. Of those that a mesh axis runs over, the one named last changes fastest.
Arguments:
- estimate: float32 [4, 1024, 3072], P('depth', 'parts', 'band'), parts along dimension 1, may hold values from 0.5 to 1.5
- psf_blocks: bfloat16 [4, 9, 361, 512], P('depth'), may hold values from 1.9520521e-06 to 0.001953125
- offset_ids: int32 [4, 9], P('depth'), may hold values from 0 to 8, as said below
- block_counts: int32 [4], P('depth'), may hold values from 1 to 9, as said below
- measured: float32 [722, 3072], P('parts', 'band'), parts along dimension 0, may hold values from 0.5 to 6
- background: float32 [722, 3072], P('parts', 'band'), parts along dimension 0, may hold values from 0.2 to 1
Outputs:
- volume: float32 [4, 1024, 3072], P('depth', 'parts', 'band'), parts along dimension 1
The draws below stay inside these ranges and needn't reach their ends.
There are 2 independent parts, one for each index of `parts`. The reference program is written for one: setup_inputs(seed, part) draws one part's arguments, and reference() takes and returns one part's arrays. A program takes and returns all parts, laid end to end along the dimension named above; an argument that names none is the same for every part. Nothing has to cross between parts.
Inputs may be any that keep to these rules, and one draw needn't show every extreme that they name: `offset_ids`: each row lists 9 distinct offset ids; the first is 4, the lenslet itself. `block_counts`: the deepest slab uses all 9 blocks.
All inputs are finite; a program needn't handle non-finite values.
Results may differ from the reference program's by a relative error of at most 0.0003.
Values may be sent and summed in bfloat16 or wider, within the bound.
No kernel may reach another device: no remote copies, remote signals or barrier semaphores. Data moves between devices by JAX's collectives and lax.ppermute only.
A program may use at most 64 MiB of HBM per device.

```python
import math
import jax
import jax.numpy as jnp
from jax import lax

PIX = 361
VOX = 512
OFFS = 9
Z = 4
ITERS = 2
LX = 96
LY = 32
LENS = 3072


def draw_offset_ids(key, part):
    key = jax.random.fold_in(key, 11)
    others = jnp.array([0, 1, 2, 3, 5, 6, 7, 8], dtype=jnp.int32)
    keys = jax.random.split(key, Z)
    shuffled = jax.vmap(lambda k: jax.random.permutation(k, others))(keys)
    center = jnp.full((Z, 1), 4, dtype=jnp.int32)
    return jnp.concatenate([center, shuffled], axis=1).astype(jnp.int32)


def draw_block_counts(key, part):
    key = jax.random.fold_in(key, 23)
    counts = jax.random.randint(key, (Z,), 1, OFFS + 1).astype(jnp.int32)
    return counts.at[Z - 1].set(OFFS)


def block_levels(key, shape, cuts, least, top_value):
    factor_of, own = 1.0, jax.random.fold_in(key, 6)
    for position, parts in cuts:
        steps = jnp.exp(jax.random.uniform(jax.random.fold_in(own, position), (parts,), jnp.float32, least / len(cuts), top_value / len(cuts)))
        factor_of = factor_of * jnp.repeat(steps, shape[position] // parts).reshape([-1 if axis == position else 1 for axis in range(len(shape))])
    return factor_of


def setup_inputs(seed: int = 0, part: int = 0) -> dict:
    splits = jax.random.split(jax.random.key(seed), 7)
    part_splits = jax.random.split(jax.random.fold_in(splits[6], part), 7)
    return {
        "estimate": jnp.clip(0.5 + 1.0 * jax.random.uniform(part_splits[0], (Z, VOX, LENS), jnp.float32) ** block_levels(part_splits[0], (Z, VOX, LENS), ((0, 2), (2, 8)), -0.2, 0.2), 0.5, 1.5),
        "psf_blocks": jnp.clip(jnp.exp(math.log(0.001953125) - 6.9083047 * jax.random.uniform(splits[1], (Z, OFFS, PIX, VOX), jnp.float32) ** block_levels(splits[1], (Z, OFFS, PIX, VOX), ((0, 2),), -0.2, 0.2)), 1.952052116394043e-06, 0.001953125).astype(jnp.bfloat16),
        "offset_ids": draw_offset_ids(jax.random.fold_in(splits[6], 71), part),
        "block_counts": draw_block_counts(jax.random.fold_in(splits[6], 71), part),
        "measured": jnp.clip(0.5 + 5.5 * jax.random.uniform(part_splits[4], (PIX, LENS), jnp.float32) ** block_levels(part_splits[4], (PIX, LENS), ((1, 8),), -0.2, 0.2), 0.5, 6.0),
        "background": jnp.clip(0.2 + 0.8 * jax.random.uniform(part_splits[5], (PIX, LENS), jnp.float32) ** block_levels(part_splits[5], (PIX, LENS), ((1, 8),), -0.2, 0.2), 0.2, 1.0),
    }


def offset_of(ident):
    return ident // 3 - 1, ident % 3 - 1


def sensitivity_of(psf_blocks, offset_ids, block_counts):
    colsum = jnp.sum(psf_blocks.astype(jnp.float32), axis=2)
    rows = jnp.arange(LY, dtype=jnp.int32)[None, None, :, None]
    cols = jnp.arange(LX, dtype=jnp.int32)[None, None, None, :]
    shift_y, shift_x = offset_of(offset_ids)
    shift_y = shift_y[:, :, None, None]
    shift_x = shift_x[:, :, None, None]
    inside = (rows - shift_y >= 0) & (rows - shift_y < LY) & (cols - shift_x >= 0) & (cols - shift_x < LX)
    active = (jnp.arange(OFFS, dtype=jnp.int32)[None, :] < block_counts[:, None])[:, :, None, None]
    valid = jnp.where(inside & active, 1.0, 0.0).astype(jnp.float32).reshape(Z, OFFS, LY * LX)
    return jnp.einsum("zov,zol->zvl", colsum, valid, precision=lax.Precision.HIGHEST)


def reference(estimate, psf_blocks, offset_ids, block_counts, measured, background):
    sensitivity = sensitivity_of(psf_blocks, offset_ids, block_counts)
    volume = estimate
    for step in range(ITERS):
        rounded = volume.astype(jnp.bfloat16).reshape(Z, VOX, LY, LX)
        padded = jnp.pad(rounded, ((0, 0), (0, 0), (1, 1), (1, 1)))
        projected = jnp.zeros((PIX, LY * LX), jnp.float32)
        for plane in range(Z):
            def add_block(slot, total, plane=plane):
                block = psf_blocks[plane, slot]
                shift_y, shift_x = offset_of(offset_ids[plane, slot])
                source = lax.dynamic_slice(padded[plane], (jnp.int32(0), (1 + shift_y).astype(jnp.int32), (1 + shift_x).astype(jnp.int32)), (VOX, LY, LX))
                return total + jnp.dot(block, source.reshape(VOX, LY * LX), preferred_element_type=jnp.float32)
            projected = lax.fori_loop(0, block_counts[plane], add_block, projected)
        ratio = (measured / (projected + background)).astype(jnp.bfloat16)
        ratio_pad = jnp.pad(ratio.reshape(PIX, LY, LX), ((0, 0), (1, 1), (1, 1)))
        planes = []
        for plane in range(Z):
            def add_back(slot, total, plane=plane):
                block = psf_blocks[plane, slot]
                shift_y, shift_x = offset_of(offset_ids[plane, slot])
                source = lax.dynamic_slice(ratio_pad, (jnp.int32(0), (1 - shift_y).astype(jnp.int32), (1 - shift_x).astype(jnp.int32)), (PIX, LY, LX))
                return total + jnp.dot(block.T, source.reshape(PIX, LY * LX), preferred_element_type=jnp.float32)
            planes.append(lax.fori_loop(0, block_counts[plane], add_back, jnp.zeros((VOX, LY * LX), jnp.float32)))
        back = jnp.stack(planes)
        volume = volume * back / sensitivity
    return volume
```

```python
import functools
import jax
import jax.numpy as jnp
from jax import lax
from jax.experimental import pallas as pl
from jax.experimental.pallas import tpu as pltpu
from jax.sharding import PartitionSpec as P

LX = 96
BF = jnp.bfloat16
F32 = jnp.float32
MAIN = 256
PADW = 384
TAIL = PADW - MAIN

SMEM = pl.BlockSpec(memory_space=pltpu.SMEM)
VMEM = pl.BlockSpec(memory_space=pltpu.VMEM)
ANY = pl.BlockSpec(memory_space=pl.ANY)


def dot(a, b):
    return lax.dot_general(a, b, (((1,), (0,)), ((), ())), preferred_element_type=F32)


def dot_t(a, b):
    return lax.dot_general(a, b, (((1,), (1,)), ((), ())), preferred_element_type=F32)


def place(ids, counts, plane, slot):
    ident = ids[plane, jnp.minimum(slot, ids.shape[1] - 1)]
    start = pl.multiple_of((2 - ident // 3) * LX, LX)
    return start, jnp.where(slot < counts[plane], ident % 3, 3)


def pair_blocks(kp, plane, a):
    tails = kp[plane, pl.ds(a, 2), MAIN:PADW, :].reshape(2 * TAIL, kp.shape[3])
    return jnp.concatenate([kp[plane, a, 0:MAIN, :], kp[plane, a + 1, 0:MAIN, :], tails], axis=0)


def project_pair(ids, counts, plane, p, x, kp, acc):
    rows = x.shape[0]
    row_a, dx_a = place(ids, counts, plane, 2 * p)
    row_b, dx_b = place(ids, counts, plane, 2 * p + 1)
    out = dot_t(x, pair_blocks(kp, plane, 2 * p))
    acc[dx_a, pl.ds(row_a, rows), 0:MAIN] += out[:, 0:MAIN]
    acc[dx_b, pl.ds(row_b, rows), 0:MAIN] += out[:, MAIN : 2 * MAIN]
    acc[dx_a, pl.ds(row_a, rows), MAIN:PADW] += out[:, 2 * MAIN : 2 * MAIN + TAIL]
    acc[dx_b, pl.ds(row_b, rows), MAIN:PADW] += out[:, 2 * MAIN + TAIL :]


def column_of(rows, width):
    return lax.rem(lax.broadcasted_iota(jnp.int32, (rows, width), 0), LX)


def fold_dx(acc):
    rows = acc.shape[1]
    col = column_of(rows, PADW)
    left = jnp.where(col > 0, pltpu.roll(acc[0], 1, 0), 0.0)
    right = jnp.where(col < LX - 1, pltpu.roll(acc[2], rows - 1, 0), 0.0)
    return acc[1] + left + right


def first_kernel(ids, counts, est, psf, part_out, est_out, kp, kraw, ev, xs, acc, ksem, esem):
    planes = est.shape[0]
    slots, pix = psf.shape[0], psf.shape[1]
    kcopies = [pltpu.make_async_copy(psf.at[s], kraw.at[s], ksem.at[s]) for s in range(slots)]
    ecopies = [pltpu.make_async_copy(est.at[z], ev.at[z], esem.at[z]) for z in range(planes)]
    kcopies[0].start()
    kcopies[1].start()
    for c in ecopies:
        c.start()
    for c in kcopies[2:]:
        c.start()
    acc[0:3] = jnp.zeros((3,) + acc.shape[1:], F32)
    full = pix // 16 * 16
    kp[:, :, full:PADW, :] = jnp.zeros(kp.shape[:2] + (PADW - full, kp.shape[3]), BF)
    if slots % 2:
        kp[:, slots, 0:full, :] = jnp.zeros((planes, full, kp.shape[3]), BF)

    def split(s):
        both = jnp.swapaxes(kraw[s], 0, 1)
        for z in range(planes):
            kp[z, s, 0:pix, :] = both[z]

    for s in range(2):
        kcopies[s].wait()
        split(s)
    for z in range(planes):
        ecopies[z].wait()
        t = ev[z].T
        est_out[z] = t
        xs[z] = t.astype(BF)
    pairs = kp.shape[1] // 2
    for p in range(pairs):
        for s in (2 * p + 2, 2 * p + 3):
            if s < slots:
                kcopies[s].wait()
        for s in (2 * p + 2, 2 * p + 3):
            if s < slots:
                split(s)
        for z in range(planes):
            project_pair(ids, counts, z, p, xs[z], kp, acc)
    part_out[...] = fold_dx(acc)


def first_call(estimate, psf, ids, counts):
    planes, vox, lens = estimate.shape
    slots, pix = psf.shape[1:3]
    rows = lens + 2 * LX
    even = slots + slots % 2
    return pl.pallas_call(
        first_kernel,
        out_shape=(
            jax.ShapeDtypeStruct((rows, PADW), F32),
            jax.ShapeDtypeStruct((planes, lens, vox), F32),
            jax.ShapeDtypeStruct((planes, even, PADW, vox), BF),
        ),
        in_specs=[SMEM, SMEM, ANY, ANY],
        out_specs=(VMEM, VMEM, VMEM),
        scratch_shapes=[
            pltpu.VMEM((slots, pix, planes, vox), BF),
            pltpu.VMEM((planes, vox, lens), F32),
            pltpu.VMEM((planes, lens, vox), BF),
            pltpu.VMEM((4, rows, PADW), F32),
            pltpu.SemaphoreType.DMA((slots,)),
            pltpu.SemaphoreType.DMA((planes,)),
        ],
        compiler_params=pltpu.CompilerParams(vmem_limit_bytes=36 << 20),
        name="project_first",
    )(ids, counts, estimate, jnp.transpose(psf, (1, 2, 0, 3)))


def sensor_kernel(meas, bg, out):
    pix = meas.shape[0]
    out[...] = jnp.zeros(out.shape, F32)
    out[0, :, 0:pix] = meas[...].T
    out[1, :, 0:pix] = bg[...].T


def sensor_call(measured, background):
    lens = measured.shape[1]
    return pl.pallas_call(
        sensor_kernel,
        out_shape=jax.ShapeDtypeStruct((2, lens, PADW), F32),
        in_specs=[VMEM, VMEM],
        out_specs=VMEM,
        compiler_params=pltpu.CompilerParams(vmem_limit_bytes=16 << 20),
        name="sensor_turn",
    )(measured, background)


def upward():
    return lax.rem(lax.axis_index("band") + lax.axis_index("depth"), 2) == 0


def edge_kernel(own, other, *refs):
    sensor, out = (refs[0], refs[1]) if len(refs) == 2 else (None, refs[0])
    rows = own.shape[0]
    up = upward()
    outer = pl.multiple_of(jnp.where(up, rows - LX, 0), LX)
    inner = pl.multiple_of(jnp.where(up, rows - 2 * LX, LX), LX)
    for i, start in enumerate((outer, inner)):
        out[i] = (own[pl.ds(start, LX), :] + other[pl.ds(start, LX), :]).astype(BF)
    if sensor is not None:
        line = pl.multiple_of(inner - LX, LX)
        for i in range(2):
            out[2 + i] = sensor[i, pl.ds(line, LX), :].astype(BF)


def edge_call(own, other, *sensor):
    return pl.pallas_call(
        edge_kernel,
        out_shape=jax.ShapeDtypeStruct((2 + 2 * len(sensor), LX, PADW), BF),
        in_specs=[VMEM] * (2 + len(sensor)),
        out_specs=VMEM,
        compiler_params=pltpu.CompilerParams(vmem_limit_bytes=16 << 20),
        name="edge_rows",
    )(own, other, *sensor)


def ratio_planes(own, other, mine, theirs, sensor, halo, planes_ref, pix):
    rows = own.shape[0]
    lens = rows - 2 * LX
    band = lax.axis_index("band")
    up = upward()
    upper = [jnp.where(up, mine[i].astype(F32), theirs[i].astype(F32)) for i in range(2)]
    lower = [jnp.where(up, theirs[i].astype(F32), mine[i].astype(F32)) for i in range(2)]
    lane = lax.broadcasted_iota(jnp.int32, (1, PADW), 1) < pix

    def ratio(start, size, extra, measured, background, there):
        total = own[start : start + size, :] + other[start : start + size, :]
        if extra is not None:
            total = total + extra
        keep = lane if there is None else jnp.logical_and(lane, there)
        return jnp.where(keep, measured / (total + background), 0.0).astype(BF).astype(F32)

    parts = [
        ratio(0, LX, lower[1], halo[0], halo[1], band > 0),
        ratio(LX, LX, lower[0], sensor[0, 0:LX], sensor[1, 0:LX], None),
        ratio(2 * LX, lens - 2 * LX, None, sensor[0, LX : lens - LX], sensor[1, LX : lens - LX], None),
        ratio(lens, LX, upper[0], sensor[0, lens - LX : lens], sensor[1, lens - LX : lens], None),
        ratio(lens + LX, LX, upper[1], halo[2], halo[3], band < lax.axis_size("band") - 1),
    ]
    whole = jnp.concatenate(parts, axis=0)
    col = column_of(rows, PADW)
    planes_ref[1] = whole.astype(BF)
    planes_ref[2] = jnp.where(col > 0, pltpu.roll(whole, 1, 0), 0.0).astype(BF)
    planes_ref[0] = jnp.where(col < LX - 1, pltpu.roll(whole, rows - 1, 0), 0.0).astype(BF)
    planes_ref[3] = jnp.zeros((rows, PADW), BF)


def back_slab(ids, counts, plane, ratios, kp, acc, colsum):
    lens = acc.shape[0]
    acc[...] = jnp.zeros(acc.shape, F32)
    if colsum is not None:
        colsum[...] = jnp.zeros(colsum.shape, F32)
        row = lax.broadcasted_iota(jnp.int32, (16, 2 * MAIN + 2 * TAIL), 0)
        lane = lax.broadcasted_iota(jnp.int32, (16, 2 * MAIN + 2 * TAIL), 1)
        first = jnp.logical_or(lane < MAIN, jnp.logical_and(lane >= 2 * MAIN, lane < 2 * MAIN + TAIL))
        ones = jnp.where(row == jnp.where(first, 0, 1), 1.0, 0.0).astype(BF)

    def pair(p, carry):
        row_a, dx_a = place(ids, counts, plane, 2 * p)
        row_b, dx_b = place(ids, counts, plane, 2 * p + 1)
        a = ratios[dx_a, pl.ds(row_a, lens), :]
        b = ratios[dx_b, pl.ds(row_b, lens), :]
        left = jnp.concatenate([a[:, 0:MAIN], b[:, 0:MAIN], a[:, MAIN:], b[:, MAIN:]], axis=1)
        if colsum is not None:
            left = jnp.concatenate([left, ones], axis=0)
        out = dot(left, pair_blocks(kp, plane, 2 * p))
        acc[...] += out[0:lens]
        if colsum is not None:
            colsum[p] = out[lens : lens + 8]
        return carry

    lax.fori_loop(0, (counts[plane] + 1) // 2, pair, 0)


def sensitivity_slab(ids, counts, plane, lens, colsum):
    groups = colsum.shape[0] * 8
    sums = colsum[...].reshape(groups, colsum.shape[2])
    high = sums.astype(BF)
    rest = sums - high.astype(F32)
    mid = rest.astype(BF)
    low = (rest - mid.astype(F32)).astype(BF)
    right = jnp.concatenate([high.astype(F32), mid.astype(F32), low.astype(F32)], axis=0)
    right = jnp.concatenate([right, jnp.zeros((128 - 3 * groups, right.shape[1]), F32)], axis=0).astype(BF)
    lane = lax.broadcasted_iota(jnp.int32, (1, 128), 1)
    place_of = lax.rem(lane, groups)
    dy = jnp.full((1, 128), 2, jnp.int32)
    dx = jnp.full((1, 128), 2, jnp.int32)
    active = jnp.zeros((1, 128), jnp.int32)
    for s in range(ids.shape[1]):
        here = place_of == (s // 2) * 8 + s % 2
        ident = ids[plane, s]
        dy = jnp.where(here, ident // 3 - 1, dy)
        dx = jnp.where(here, ident % 3 - 1, dx)
        active = jnp.where(here, (s < counts[plane]).astype(jnp.int32), active)
    active = jnp.where(lane < 3 * groups, active, 0)
    l = lax.broadcasted_iota(jnp.int32, (lens, 128), 0)
    grid_rows = lens // LX * lax.axis_size("band")
    row = lax.axis_index("band") * (lens // LX) + l // LX - dy
    col = lax.rem(l, LX) - dx
    inside = (row >= 0) & (row < grid_rows) & (col >= 0) & (col < LX) & (active > 0)
    return dot(jnp.where(inside, 1.0, 0.0).astype(BF), right)


def middle_kernel(pix, ids, counts, own, other, mine, theirs, sensor, est, kp, part_out, vol_out, inv_out, halo_out, ratios, xs, back, colsum, acc):
    up = upward()
    for i in range(2):
        a = mine[2 + i].astype(F32)
        b = theirs[2 + i].astype(F32)
        halo_out[i] = jnp.where(up, b, a)
        halo_out[2 + i] = jnp.where(up, a, b)
    ratio_planes(own, other, mine, theirs, sensor, halo_out, ratios, pix)
    acc[0:3] = jnp.zeros((3,) + acc.shape[1:], F32)
    lens = est.shape[1]
    for z in range(est.shape[0]):
        back_slab(ids, counts, z, ratios, kp, back, colsum)
        inv = 1.0 / sensitivity_slab(ids, counts, z, lens, colsum)
        inv_out[z] = inv
        vol = est[z] * back[...] * inv
        vol_out[z] = vol
        xs[...] = vol.astype(BF)

        def pair(p, carry, z=z):
            project_pair(ids, counts, z, p, xs[...], kp, acc)
            return carry

        lax.fori_loop(0, (counts[z] + 1) // 2, pair, 0)
    part_out[...] = fold_dx(acc)


def middle_call(pix, ids, counts, own, other, mine, theirs, sensor, est, kp):
    planes, lens, vox = est.shape
    rows = own.shape[0]
    return pl.pallas_call(
        functools.partial(middle_kernel, pix),
        out_shape=(
            jax.ShapeDtypeStruct((rows, PADW), F32),
            jax.ShapeDtypeStruct((planes, lens, vox), F32),
            jax.ShapeDtypeStruct((planes, lens, vox), F32),
            jax.ShapeDtypeStruct((4, LX, PADW), F32),
        ),
        in_specs=[SMEM, SMEM] + [VMEM] * 7,
        out_specs=(VMEM,) * 4,
        scratch_shapes=[
            pltpu.VMEM((4, rows, PADW), BF),
            pltpu.VMEM((lens, vox), BF),
            pltpu.VMEM((lens, vox), F32),
            pltpu.VMEM((kp.shape[1] // 2, 8, vox), F32),
            pltpu.VMEM((4, rows, PADW), F32),
        ],
        compiler_params=pltpu.CompilerParams(vmem_limit_bytes=36 << 20),
        name="back_and_project",
    )(ids, counts, own, other, mine, theirs, sensor, est, kp)


def last_kernel(pix, ids, counts, own, other, mine, theirs, sensor, halo, vol, inv, kp, out, ratios, back):
    ratio_planes(own, other, mine, theirs, sensor, halo, ratios, pix)
    for z in range(vol.shape[0]):
        back_slab(ids, counts, z, ratios, kp, back, None)
        out[z] = (vol[z] * back[...] * inv[z]).T


def last_call(pix, ids, counts, own, other, mine, theirs, sensor, halo, vol, inv, kp):
    planes, lens, vox = vol.shape
    rows = own.shape[0]
    return pl.pallas_call(
        functools.partial(last_kernel, pix),
        out_shape=jax.ShapeDtypeStruct((planes, vox, lens), F32),
        in_specs=[SMEM, SMEM] + [VMEM] * 9,
        out_specs=VMEM,
        scratch_shapes=[
            pltpu.VMEM((4, rows, PADW), BF),
            pltpu.VMEM((lens, vox), F32),
        ],
        compiler_params=pltpu.CompilerParams(vmem_limit_bytes=36 << 20),
        name="back_last",
    )(ids, counts, own, other, mine, theirs, sensor, halo, vol, inv, kp)


def swap(x):
    return lax.ppermute(x, "depth", [(0, 1), (1, 0)])


def edge_exchange(x):
    bands = lax.axis_size("band")
    pairs = []
    for b in range(bands - 1):
        d = b % 2
        pairs += [(2 * b + d, 2 * b + 2 + d), (2 * b + 2 + d, 2 * b + d)]
    return lax.ppermute(x, ("band", "depth"), pairs)


def per_device(estimate, psf_blocks, offset_ids, block_counts, measured, background):
    pix = measured.shape[0]
    part, est, kp = first_call(estimate, psf_blocks, offset_ids, block_counts)
    other = swap(part)
    sensor = sensor_call(measured, background)
    mine = edge_exchange(edge_call(part, other, sensor))
    theirs = swap(mine)
    part, vol, inv, halo = middle_call(pix, offset_ids, block_counts, part, other, mine, theirs, sensor, est, kp)
    other = swap(part)
    mine = edge_exchange(edge_call(part, other))
    theirs = swap(mine)
    return last_call(pix, offset_ids, block_counts, part, other, mine, theirs, sensor, halo, vol, inv, kp)


def solution(mesh):
    in_specs = (
        P("depth", "parts", "band"),
        P("depth", None, None, None),
        P("depth", None),
        P("depth"),
        P("parts", "band"),
        P("parts", "band"),
    )
    return jax.shard_map(
        per_device, mesh=mesh, in_specs=in_specs, out_specs=P("depth", "parts", "band"), check_vma=False
    )
```

```python
import functools
import jax
import jax.numpy as jnp
from jax import lax
from jax.experimental import pallas as pl
from jax.experimental.pallas import tpu as pltpu
from jax.sharding import PartitionSpec as P

LX = 96
BF = jnp.bfloat16
F32 = jnp.float32
PADW = 384
SPLIT_VMEM = 24 << 20

SMEM = pl.BlockSpec(memory_space=pltpu.SMEM)
VMEM = pl.BlockSpec(memory_space=pltpu.VMEM)
ANY = pl.BlockSpec(memory_space=pl.ANY)


def dot(a, b):
    return lax.dot_general(a, b, (((1,), (0,)), ((), ())), preferred_element_type=F32)


def dot_t(a, b):
    return lax.dot_general(a, b, (((1,), (1,)), ((), ())), preferred_element_type=F32)


def count_of(info, plane):
    return info[1][plane]


def place(info, plane, slot):
    ident = info[0][plane, min(slot, info[0].shape[1] - 1)]
    start = pl.multiple_of((2 - ident // 3) * LX, LX)
    return start, jnp.where(slot < count_of(info, plane), ident % 3, 3)


def by_pairs(info, plane, slots, body):
    pairs = (count_of(info, plane) + 1) // 2
    for k in range(1, slots // 2 + 1):
        pl.when(pairs == k)(functools.partial(body, 2 * k))


def project_slab(info, plane, x, kp, acc):
    rows, vox = x.shape

    def body(used):
        out = dot_t(x[...], kp[plane, 0:used].reshape(used * PADW, vox))
        for s in range(used):
            row, dx = place(info, plane, s)
            acc[dx, pl.ds(row, rows), :] += out[:, s * PADW : (s + 1) * PADW]

    by_pairs(info, plane, kp.shape[1], body)


def back_slab(info, plane, ratios, kp, acc):
    lens, vox = acc.shape

    def body(used):
        left = []
        for s in range(used):
            row, dx = place(info, plane, s)
            left.append(ratios[dx, pl.ds(row, lens), :])
        acc[...] = dot(jnp.concatenate(left, axis=1), kp[plane, 0:used].reshape(used * PADW, vox))

    by_pairs(info, plane, kp.shape[1], body)


def each_plane(planes, body):
    lax.fori_loop(0, planes, lambda z, carry: (body(z), carry)[1], 0)


def column_of(rows, width):
    return lax.rem(lax.broadcasted_iota(jnp.int32, (rows, width), 0), LX)


def fold_dx(acc):
    rows = acc.shape[1]
    col = column_of(rows, PADW)
    left = jnp.where(col > 0, pltpu.roll(acc[0], 1, 0), 0.0)
    right = jnp.where(col < LX - 1, pltpu.roll(acc[2], rows - 1, 0), 0.0)
    return acc[1] + left + right


def split_kernel(psf, kp):
    slots, pix, planes, vox = psf.shape
    even = kp.shape[1]
    full = pix // 16 * 16
    kp[:, :, full:PADW, :] = jnp.zeros((planes, even, PADW - full, vox), BF)
    if slots < even:
        kp[:, slots, 0:full, :] = jnp.zeros((planes, full, vox), BF)
    for s in range(slots):
        both = jnp.swapaxes(psf[s], 0, 1)
        for z in range(planes):
            kp[z, s, 0:pix, :] = both[z]


def split_call(psf):
    planes, slots, pix, vox = psf.shape
    return pl.pallas_call(
        split_kernel,
        out_shape=jax.ShapeDtypeStruct((planes, slots + slots % 2, PADW, vox), BF),
        in_specs=[VMEM],
        out_specs=VMEM,
        compiler_params=pltpu.CompilerParams(vmem_limit_bytes=SPLIT_VMEM),
        cost_estimate=cost(5),
        name="split_planes",
    )(jnp.transpose(psf, (1, 2, 0, 3)))


def first_kernel(ids, counts, est, kp, part_out, est_out, xs, acc):
    acc[0:3] = jnp.zeros((3,) + acc.shape[1:], F32)

    def body(z):
        t = est[z].T
        est_out[z] = t
        xs[...] = t.astype(BF)
        project_slab((ids, counts), z, xs, kp, acc)

    each_plane(est.shape[0], body)
    part_out[...] = fold_dx(acc)


def first_call(estimate, kp, ids, counts):
    planes, vox, lens = estimate.shape
    rows = lens + 2 * LX
    return pl.pallas_call(
        first_kernel,
        out_shape=(
            jax.ShapeDtypeStruct((rows, PADW), F32),
            jax.ShapeDtypeStruct((planes, lens, vox), F32),
        ),
        in_specs=[SMEM, SMEM, VMEM, VMEM],
        out_specs=(VMEM, VMEM),
        scratch_shapes=[
            pltpu.VMEM((lens, vox), BF),
            pltpu.VMEM((4, rows, PADW), F32),
        ],
        compiler_params=pltpu.CompilerParams(vmem_limit_bytes=36 << 20),
        cost_estimate=cost(5),
        name="project_first",
    )(ids, counts, estimate, kp)


def cost(us):
    return pl.CostEstimate(flops=int(us * 1e9), bytes_accessed=int(us * 3e6), transcendentals=0)


def sensor_kernel(meas, bg, out):
    pix = meas.shape[0]
    out[...] = jnp.zeros(out.shape, F32)
    out[0, :, 0:pix] = meas[...].T
    out[1, :, 0:pix] = bg[...].T


def sensor_call(measured, background):
    lens = measured.shape[1]
    return pl.pallas_call(
        sensor_kernel,
        out_shape=jax.ShapeDtypeStruct((2, lens, PADW), F32),
        in_specs=[VMEM, VMEM],
        out_specs=VMEM,
        compiler_params=pltpu.CompilerParams(vmem_limit_bytes=16 << 20),
        cost_estimate=cost(1),
        name="sensor_turn",
    )(measured, background)


def upward():
    return lax.rem(lax.axis_index("band") + lax.axis_index("depth"), 2) == 0


def edge_kernel(own, other, *refs):
    sensor, out = (refs[0], refs[1]) if len(refs) == 2 else (None, refs[0])
    rows = own.shape[0]
    up = upward()
    outer = pl.multiple_of(jnp.where(up, rows - LX, 0), LX)
    inner = pl.multiple_of(jnp.where(up, rows - 2 * LX, LX), LX)
    for i, start in enumerate((outer, inner)):
        out[i] = (own[pl.ds(start, LX), :] + other[pl.ds(start, LX), :]).astype(BF)
    if sensor is not None:
        line = pl.multiple_of(inner - LX, LX)
        for i in range(2):
            out[2 + i] = sensor[i, pl.ds(line, LX), :].astype(BF)


def edge_call(own, other, *sensor):
    return pl.pallas_call(
        edge_kernel,
        out_shape=jax.ShapeDtypeStruct((2 + 2 * len(sensor), LX, PADW), BF),
        in_specs=[VMEM] * (2 + len(sensor)),
        out_specs=VMEM,
        compiler_params=pltpu.CompilerParams(vmem_limit_bytes=16 << 20),
        name="edge_rows",
    )(own, other, *sensor)


def ratio_planes(own, other, mine, theirs, sensor, halo, planes_ref, pix):
    rows = own.shape[0]
    lens = rows - 2 * LX
    band = lax.axis_index("band")
    up = upward()
    upper = [jnp.where(up, mine[i].astype(F32), theirs[i].astype(F32)) for i in range(2)]
    lower = [jnp.where(up, theirs[i].astype(F32), mine[i].astype(F32)) for i in range(2)]
    lane = lax.broadcasted_iota(jnp.int32, (1, PADW), 1) < pix

    def ratio(start, size, extra, measured, background, there):
        total = own[start : start + size, :] + other[start : start + size, :]
        if extra is not None:
            total = total + extra
        keep = lane if there is None else jnp.logical_and(lane, there)
        return jnp.where(keep, measured / (total + background), 0.0).astype(BF).astype(F32)

    parts = [
        ratio(0, LX, lower[1], halo[0], halo[1], band > 0),
        ratio(LX, LX, lower[0], sensor[0, 0:LX], sensor[1, 0:LX], None),
        ratio(2 * LX, lens - 2 * LX, None, sensor[0, LX : lens - LX], sensor[1, LX : lens - LX], None),
        ratio(lens, LX, upper[0], sensor[0, lens - LX : lens], sensor[1, lens - LX : lens], None),
        ratio(lens + LX, LX, upper[1], halo[2], halo[3], band < lax.axis_size("band") - 1),
    ]
    whole = jnp.concatenate(parts, axis=0)
    col = column_of(rows, PADW)
    planes_ref[1] = whole.astype(BF)
    planes_ref[2] = jnp.where(col > 0, pltpu.roll(whole, 1, 0), 0.0).astype(BF)
    planes_ref[0] = jnp.where(col < LX - 1, pltpu.roll(whole, rows - 1, 0), 0.0).astype(BF)
    planes_ref[3] = jnp.zeros((rows, PADW), BF)


def sensitivity_kernel(ids, counts, kp, after, inv_out):
    planes, even, _, vox = kp.shape
    lens = inv_out.shape[1]
    width = even * PADW
    lane = lax.broadcasted_iota(jnp.int32, (16, width), 1)
    slot = lax.broadcasted_iota(jnp.int32, (16, width), 0)
    ones = jnp.where(lane // PADW == slot, 1.0, 0.0).astype(BF)
    lane = lax.broadcasted_iota(jnp.int32, (1, 128), 1)
    slot = lax.rem(lane, 16)
    l = lax.broadcasted_iota(jnp.int32, (lens, 128), 0)
    grid_rows = lens // LX * lax.axis_size("band")
    row = lax.axis_index("band") * (lens // LX) + l // LX
    col = lax.rem(l, LX)

    def body(z):
        sums = dot(ones, kp[z].reshape(width, vox))
        high = sums.astype(BF).astype(F32)
        mid = (sums - high).astype(BF).astype(F32)
        low = sums - high - mid
        right = jnp.concatenate([high, mid, low, jnp.zeros((80, vox), F32)], axis=0).astype(BF)
        dy = jnp.zeros((1, 128), jnp.int32)
        dx = jnp.zeros((1, 128), jnp.int32)
        for s in range(ids.shape[1]):
            dy = jnp.where(slot == s, ids[z, s] // 3 - 1, dy)
            dx = jnp.where(slot == s, ids[z, s] % 3 - 1, dx)
        active = (slot < counts[z]) & (lane < 48)
        r = row - dy
        c = col - dx
        inside = (r >= 0) & (r < grid_rows) & (c >= 0) & (c < LX) & active
        inv_out[z] = 1.0 / dot(jnp.where(inside, 1.0, 0.0).astype(BF), right)

    each_plane(planes, body)


def sensitivity_call(ids, counts, kp, lens, after):
    planes, _, _, vox = kp.shape
    return pl.pallas_call(
        sensitivity_kernel,
        out_shape=jax.ShapeDtypeStruct((planes, lens, vox), F32),
        in_specs=[SMEM, SMEM, VMEM, ANY],
        out_specs=VMEM,
        compiler_params=pltpu.CompilerParams(vmem_limit_bytes=16 << 20),
        cost_estimate=cost(3),
        name="sensitivity",
    )(ids, counts, kp, after)


def middle_kernel(pix, ids, counts, own, other, mine, theirs, sensor, est, inv, kp, part_out, vol_out, halo_out, ratios, xs, back, acc):
    up = upward()
    for i in range(2):
        a = mine[2 + i].astype(F32)
        b = theirs[2 + i].astype(F32)
        halo_out[i] = jnp.where(up, b, a)
        halo_out[2 + i] = jnp.where(up, a, b)
    ratio_planes(own, other, mine, theirs, sensor, halo_out, ratios, pix)
    acc[0:3] = jnp.zeros((3,) + acc.shape[1:], F32)

    def body(z):
        back_slab((ids, counts), z, ratios, kp, back)
        vol = est[z] * back[...] * inv[z]
        vol_out[z] = vol
        xs[...] = vol.astype(BF)
        project_slab((ids, counts), z, xs, kp, acc)

    each_plane(est.shape[0], body)
    part_out[...] = fold_dx(acc)


def middle_call(pix, ids, counts, own, other, mine, theirs, sensor, est, inv, kp):
    planes, lens, vox = est.shape
    rows = own.shape[0]
    return pl.pallas_call(
        functools.partial(middle_kernel, pix),
        out_shape=(
            jax.ShapeDtypeStruct((rows, PADW), F32),
            jax.ShapeDtypeStruct((planes, lens, vox), F32),
            jax.ShapeDtypeStruct((4, LX, PADW), F32),
        ),
        in_specs=[SMEM, SMEM] + [VMEM] * 8,
        out_specs=(VMEM,) * 3,
        scratch_shapes=[
            pltpu.VMEM((4, rows, PADW), BF),
            pltpu.VMEM((lens, vox), BF),
            pltpu.VMEM((lens, vox), F32),
            pltpu.VMEM((4, rows, PADW), F32),
        ],
        compiler_params=pltpu.CompilerParams(vmem_limit_bytes=36 << 20),
        cost_estimate=cost(10),
        name="back_and_project",
    )(ids, counts, own, other, mine, theirs, sensor, est, inv, kp)


def last_kernel(pix, ids, counts, own, other, mine, theirs, sensor, halo, vol, inv, kp, out, ratios, back):
    ratio_planes(own, other, mine, theirs, sensor, halo, ratios, pix)

    def body(z):
        back_slab((ids, counts), z, ratios, kp, back)
        out[z] = (vol[z] * back[...] * inv[z]).T

    each_plane(vol.shape[0], body)


def last_call(pix, ids, counts, own, other, mine, theirs, sensor, halo, vol, inv, kp):
    planes, lens, vox = vol.shape
    rows = own.shape[0]
    return pl.pallas_call(
        functools.partial(last_kernel, pix),
        out_shape=jax.ShapeDtypeStruct((planes, vox, lens), F32),
        in_specs=[SMEM, SMEM] + [VMEM] * 9,
        out_specs=VMEM,
        scratch_shapes=[
            pltpu.VMEM((4, rows, PADW), BF),
            pltpu.VMEM((lens, vox), F32),
        ],
        compiler_params=pltpu.CompilerParams(vmem_limit_bytes=36 << 20),
        cost_estimate=cost(6),
        name="back_last",
    )(ids, counts, own, other, mine, theirs, sensor, halo, vol, inv, kp)


def swap(x):
    return lax.ppermute(x, "depth", [(0, 1), (1, 0)])


def edge_exchange(x):
    bands = lax.axis_size("band")
    pairs = []
    for b in range(bands - 1):
        d = b % 2
        pairs += [(2 * b + d, 2 * b + 2 + d), (2 * b + 2 + d, 2 * b + d)]
    return lax.ppermute(x, ("band", "depth"), pairs)


def per_device(estimate, psf_blocks, offset_ids, block_counts, measured, background):
    pix, lens = measured.shape
    kp = split_call(psf_blocks)
    part, est = first_call(estimate, kp, offset_ids, block_counts)
    other = swap(part)
    sensor = sensor_call(measured, background)
    edges = edge_call(part, other, sensor)
    mine = edge_exchange(edges)
    inv = sensitivity_call(offset_ids, block_counts, kp, lens, edges)
    mine, inv = lax.optimization_barrier((mine, inv))
    theirs = swap(mine)
    part, vol, halo = middle_call(pix, offset_ids, block_counts, part, other, mine, theirs, sensor, est, inv, kp)
    other = swap(part)
    mine = edge_exchange(edge_call(part, other))
    theirs = swap(mine)
    return last_call(pix, offset_ids, block_counts, part, other, mine, theirs, sensor, halo, vol, inv, kp)


def solution(mesh):
    in_specs = (
        P("depth", "parts", "band"),
        P("depth", None, None, None),
        P("depth", None),
        P("depth"),
        P("parts", "band"),
        P("parts", "band"),
    )
    return jax.shard_map(
        per_device, mesh=mesh, in_specs=in_specs, out_specs=P("depth", "parts", "band"), check_vma=False
    )
```

```python
import functools
import jax
import jax.numpy as jnp
from jax import lax
from jax.experimental import pallas as pl
from jax.experimental.pallas import tpu as pltpu
from jax.sharding import PartitionSpec as P

LX = 96
BF = jnp.bfloat16
F32 = jnp.float32
PADW = 384
SPLIT_VMEM = 24 << 20

SMEM = pl.BlockSpec(memory_space=pltpu.SMEM)
VMEM = pl.BlockSpec(memory_space=pltpu.VMEM)
ANY = pl.BlockSpec(memory_space=pl.ANY)


def dot(a, b):
    return lax.dot_general(a, b, (((1,), (0,)), ((), ())), preferred_element_type=F32)


def dot_t(a, b):
    return lax.dot_general(a, b, (((1,), (1,)), ((), ())), preferred_element_type=F32)


def count_of(info, plane):
    return info[1][plane]


def place(info, plane, slot):
    ident = info[0][plane, min(slot, info[0].shape[1] - 1)]
    start = pl.multiple_of((2 - ident // 3) * LX, LX)
    return start, jnp.where(slot < count_of(info, plane), ident % 3, 3)


def by_pairs(info, plane, slots, body):
    pairs = (count_of(info, plane) + 1) // 2
    for k in range(1, slots // 2 + 1):
        pl.when(pairs == k)(functools.partial(body, 2 * k))


def project_slab(info, plane, x, kp, acc):
    rows, vox = x.shape

    def body(used):
        out = dot_t(x[...], kp[plane, 0:used].reshape(used * PADW, vox))
        for s in range(used):
            row, dx = place(info, plane, s)
            acc[dx, pl.ds(row, rows), :] += out[:, s * PADW : (s + 1) * PADW]

    by_pairs(info, plane, kp.shape[1], body)


def back_slab(info, plane, ratios, kp, acc):
    lens, vox = acc.shape

    def body(used):
        left = []
        for s in range(used):
            row, dx = place(info, plane, s)
            left.append(ratios[dx, pl.ds(row, lens), :])
        acc[...] = dot(jnp.concatenate(left, axis=1), kp[plane, 0:used].reshape(used * PADW, vox))

    by_pairs(info, plane, kp.shape[1], body)


def each_plane(planes, body):
    lax.fori_loop(0, planes, lambda z, carry: (body(z), carry)[1], 0)


def column_of(rows, width):
    return lax.rem(lax.broadcasted_iota(jnp.int32, (rows, width), 0), LX)


def fold_dx(acc):
    rows = acc.shape[1]
    col = column_of(rows, PADW)
    left = jnp.where(col > 0, pltpu.roll(acc[0], 1, 0), 0.0)
    right = jnp.where(col < LX - 1, pltpu.roll(acc[2], rows - 1, 0), 0.0)
    return acc[1] + left + right


def split_kernel(psf, kp):
    slots, pix, planes, vox = psf.shape
    even = kp.shape[1]
    full = pix // 16 * 16
    kp[:, :, full:PADW, :] = jnp.zeros((planes, even, PADW - full, vox), BF)
    if slots < even:
        kp[:, slots, 0:full, :] = jnp.zeros((planes, full, vox), BF)
    for s in range(slots):
        both = jnp.swapaxes(psf[s], 0, 1)
        for z in range(planes):
            kp[z, s, 0:pix, :] = both[z]


def split_call(psf):
    planes, slots, pix, vox = psf.shape
    return pl.pallas_call(
        split_kernel,
        out_shape=jax.ShapeDtypeStruct((planes, slots + slots % 2, PADW, vox), BF),
        in_specs=[VMEM],
        out_specs=VMEM,
        compiler_params=pltpu.CompilerParams(vmem_limit_bytes=SPLIT_VMEM),
        cost_estimate=cost(5),
        name="split_planes",
    )(jnp.transpose(psf, (1, 2, 0, 3)))


def first_kernel(ids, counts, est, kp, part_out, est_out, xs, acc):
    acc[0:3] = jnp.zeros((3,) + acc.shape[1:], F32)

    def body(z):
        t = est[z].T
        est_out[z] = t
        xs[...] = t.astype(BF)
        project_slab((ids, counts), z, xs, kp, acc)

    each_plane(est.shape[0], body)
    part_out[...] = fold_dx(acc)


def first_call(estimate, kp, ids, counts):
    planes, vox, lens = estimate.shape
    rows = lens + 2 * LX
    return pl.pallas_call(
        first_kernel,
        out_shape=(
            jax.ShapeDtypeStruct((rows, PADW), F32),
            jax.ShapeDtypeStruct((planes, lens, vox), F32),
        ),
        in_specs=[SMEM, SMEM, VMEM, VMEM],
        out_specs=(VMEM, VMEM),
        scratch_shapes=[
            pltpu.VMEM((lens, vox), BF),
            pltpu.VMEM((4, rows, PADW), F32),
        ],
        compiler_params=pltpu.CompilerParams(vmem_limit_bytes=36 << 20),
        cost_estimate=cost(5),
        name="project_first",
    )(ids, counts, estimate, kp)


def cost(us):
    return pl.CostEstimate(flops=int(us * 1e9), bytes_accessed=int(us * 3e6), transcendentals=0)


def sensor_kernel(meas, bg, out):
    pix = meas.shape[0]
    out[...] = jnp.zeros(out.shape, F32)
    out[0, :, 0:pix] = meas[...].T
    out[1, :, 0:pix] = bg[...].T


def sensor_call(measured, background):
    lens = measured.shape[1]
    return pl.pallas_call(
        sensor_kernel,
        out_shape=jax.ShapeDtypeStruct((2, lens, PADW), F32),
        in_specs=[VMEM, VMEM],
        out_specs=VMEM,
        compiler_params=pltpu.CompilerParams(vmem_limit_bytes=16 << 20),
        cost_estimate=cost(1),
        name="sensor_turn",
    )(measured, background)


def upward():
    return lax.rem(lax.axis_index("band") + lax.axis_index("depth"), 2) == 0


def edge_kernel(own, other, *refs):
    sensor, out = (refs[0], refs[1]) if len(refs) == 2 else (None, refs[0])
    rows = own.shape[0]
    up = upward()
    outer = pl.multiple_of(jnp.where(up, rows - LX, 0), LX)
    inner = pl.multiple_of(jnp.where(up, rows - 2 * LX, LX), LX)
    for i, start in enumerate((outer, inner)):
        out[i] = (own[pl.ds(start, LX), :] + other[pl.ds(start, LX), :]).astype(BF)
    if sensor is not None:
        line = pl.multiple_of(inner - LX, LX)
        for i in range(2):
            out[2 + i] = sensor[i, pl.ds(line, LX), :].astype(BF)


def edge_call(own, other, *sensor):
    return pl.pallas_call(
        edge_kernel,
        out_shape=jax.ShapeDtypeStruct((2 + 2 * len(sensor), LX, PADW), BF),
        in_specs=[VMEM] * (2 + len(sensor)),
        out_specs=VMEM,
        compiler_params=pltpu.CompilerParams(vmem_limit_bytes=16 << 20),
        name="edge_rows",
    )(own, other, *sensor)


def ratio_planes(own, other, mine, theirs, sensor, halo, planes_ref, pix):
    rows = own.shape[0]
    lens = rows - 2 * LX
    band = lax.axis_index("band")
    up = upward()
    upper = [jnp.where(up, mine[i].astype(F32), theirs[i].astype(F32)) for i in range(2)]
    lower = [jnp.where(up, theirs[i].astype(F32), mine[i].astype(F32)) for i in range(2)]
    below = band > 0
    above = band < lax.axis_size("band") - 1
    lane = lax.broadcasted_iota(jnp.int32, (1, PADW), 1) < pix

    def ratio(start, size, extra, measured, background, there):
        total = own[start : start + size, :] + other[start : start + size, :]
        if extra is not None:
            total = total + extra
        keep = lane if there is None else jnp.logical_and(lane, there)
        return jnp.where(keep, measured / (total + background), 0.0).astype(BF).astype(F32)

    parts = [
        ratio(0, LX, lower[1], halo[0], halo[1], below),
        ratio(LX, LX, jnp.where(below, lower[0], 0.0), sensor[0, 0:LX], sensor[1, 0:LX], None),
        ratio(2 * LX, lens - 2 * LX, None, sensor[0, LX : lens - LX], sensor[1, LX : lens - LX], None),
        ratio(lens, LX, jnp.where(above, upper[0], 0.0), sensor[0, lens - LX : lens], sensor[1, lens - LX : lens], None),
        ratio(lens + LX, LX, upper[1], halo[2], halo[3], above),
    ]
    whole = jnp.concatenate(parts, axis=0)
    col = column_of(rows, PADW)
    planes_ref[1] = whole.astype(BF)
    planes_ref[2] = jnp.where(col > 0, pltpu.roll(whole, 1, 0), 0.0).astype(BF)
    planes_ref[0] = jnp.where(col < LX - 1, pltpu.roll(whole, rows - 1, 0), 0.0).astype(BF)
    planes_ref[3] = jnp.zeros((rows, PADW), BF)


def sensitivity_kernel(ids, counts, kp, after, inv_out):
    planes, even, _, vox = kp.shape
    lens = inv_out.shape[1]
    width = even * PADW
    lane = lax.broadcasted_iota(jnp.int32, (16, width), 1)
    slot = lax.broadcasted_iota(jnp.int32, (16, width), 0)
    ones = jnp.where(lane // PADW == slot, 1.0, 0.0).astype(BF)
    lane = lax.broadcasted_iota(jnp.int32, (1, 128), 1)
    slot = lax.rem(lane, 16)
    l = lax.broadcasted_iota(jnp.int32, (lens, 128), 0)
    grid_rows = lens // LX * lax.axis_size("band")
    row = lax.axis_index("band") * (lens // LX) + l // LX
    col = lax.rem(l, LX)

    def body(z):
        sums = dot(ones, kp[z].reshape(width, vox))
        high = sums.astype(BF).astype(F32)
        mid = (sums - high).astype(BF).astype(F32)
        low = sums - high - mid
        right = jnp.concatenate([high, mid, low, jnp.zeros((80, vox), F32)], axis=0).astype(BF)
        dy = jnp.zeros((1, 128), jnp.int32)
        dx = jnp.zeros((1, 128), jnp.int32)
        for s in range(ids.shape[1]):
            dy = jnp.where(slot == s, ids[z, s] // 3 - 1, dy)
            dx = jnp.where(slot == s, ids[z, s] % 3 - 1, dx)
        active = (slot < counts[z]) & (lane < 48)
        r = row - dy
        c = col - dx
        inside = (r >= 0) & (r < grid_rows) & (c >= 0) & (c < LX) & active
        inv_out[z] = 1.0 / dot(jnp.where(inside, 1.0, 0.0).astype(BF), right)

    each_plane(planes, body)


def sensitivity_call(ids, counts, kp, lens, after):
    planes, _, _, vox = kp.shape
    return pl.pallas_call(
        sensitivity_kernel,
        out_shape=jax.ShapeDtypeStruct((planes, lens, vox), F32),
        in_specs=[SMEM, SMEM, VMEM, ANY],
        out_specs=VMEM,
        compiler_params=pltpu.CompilerParams(vmem_limit_bytes=16 << 20),
        cost_estimate=cost(3),
        name="sensitivity",
    )(ids, counts, kp, after)


def middle_kernel(pix, ids, counts, own, other, mine, theirs, sensor, est, inv, kp, part_out, vol_out, halo_out, ratios, xs, back, acc):
    up = upward()
    for i in range(2):
        a = mine[2 + i].astype(F32)
        b = theirs[2 + i].astype(F32)
        halo_out[i] = jnp.where(up, b, a)
        halo_out[2 + i] = jnp.where(up, a, b)
    ratio_planes(own, other, mine, theirs, sensor, halo_out, ratios, pix)
    acc[0:3] = jnp.zeros((3,) + acc.shape[1:], F32)

    def body(z):
        back_slab((ids, counts), z, ratios, kp, back)
        vol = est[z] * back[...] * inv[z]
        vol_out[z] = vol
        xs[...] = vol.astype(BF)
        project_slab((ids, counts), z, xs, kp, acc)

    each_plane(est.shape[0], body)
    part_out[...] = fold_dx(acc)


def middle_call(pix, ids, counts, own, other, mine, theirs, sensor, est, inv, kp):
    planes, lens, vox = est.shape
    rows = own.shape[0]
    return pl.pallas_call(
        functools.partial(middle_kernel, pix),
        out_shape=(
            jax.ShapeDtypeStruct((rows, PADW), F32),
            jax.ShapeDtypeStruct((planes, lens, vox), F32),
            jax.ShapeDtypeStruct((4, LX, PADW), F32),
        ),
        in_specs=[SMEM, SMEM] + [VMEM] * 8,
        out_specs=(VMEM,) * 3,
        scratch_shapes=[
            pltpu.VMEM((4, rows, PADW), BF),
            pltpu.VMEM((lens, vox), BF),
            pltpu.VMEM((lens, vox), F32),
            pltpu.VMEM((4, rows, PADW), F32),
        ],
        compiler_params=pltpu.CompilerParams(vmem_limit_bytes=36 << 20),
        cost_estimate=cost(10),
        name="back_and_project",
    )(ids, counts, own, other, mine, theirs, sensor, est, inv, kp)


def last_kernel(pix, ids, counts, own, other, mine, theirs, sensor, halo, vol, inv, kp, out, ratios, back):
    ratio_planes(own, other, mine, theirs, sensor, halo, ratios, pix)

    def body(z):
        back_slab((ids, counts), z, ratios, kp, back)
        out[z] = (vol[z] * back[...] * inv[z]).T

    each_plane(vol.shape[0], body)


def last_call(pix, ids, counts, own, other, mine, theirs, sensor, halo, vol, inv, kp):
    planes, lens, vox = vol.shape
    rows = own.shape[0]
    return pl.pallas_call(
        functools.partial(last_kernel, pix),
        out_shape=jax.ShapeDtypeStruct((planes, vox, lens), F32),
        in_specs=[SMEM, SMEM] + [VMEM] * 9,
        out_specs=VMEM,
        scratch_shapes=[
            pltpu.VMEM((4, rows, PADW), BF),
            pltpu.VMEM((lens, vox), F32),
        ],
        compiler_params=pltpu.CompilerParams(vmem_limit_bytes=36 << 20),
        cost_estimate=cost(6),
        name="back_last",
    )(ids, counts, own, other, mine, theirs, sensor, halo, vol, inv, kp)


def swap(x):
    return lax.ppermute(x, "depth", [(0, 1), (1, 0)])


def edge_exchange(x):
    parts, bands, depth = (lax.axis_size(a) for a in ("parts", "band", "depth"))
    pairs = []
    for p in range(parts):
        for b in range(bands):
            for d in range(depth):
                q, c = p, b + (1 if (b + d) % 2 == 0 else -1)
                if c < 0 or c == bands:
                    q, c = min(p ^ 1, parts - 1), b
                pairs.append(((p * bands + b) * depth + d, (q * bands + c) * depth + d))
    return lax.ppermute(x, ("parts", "band", "depth"), pairs)


def per_device(estimate, psf_blocks, offset_ids, block_counts, measured, background):
    pix, lens = measured.shape
    kp = split_call(psf_blocks)
    part, est = first_call(estimate, kp, offset_ids, block_counts)
    other = swap(part)
    sensor = sensor_call(measured, background)
    edges = edge_call(part, other, sensor)
    mine = edge_exchange(edges)
    inv = sensitivity_call(offset_ids, block_counts, kp, lens, edges)
    mine, inv = lax.optimization_barrier((mine, inv))
    theirs = swap(mine)
    part, vol, halo = middle_call(pix, offset_ids, block_counts, part, other, mine, theirs, sensor, est, inv, kp)
    other = swap(part)
    mine = edge_exchange(edge_call(part, other))
    theirs = swap(mine)
    return last_call(pix, offset_ids, block_counts, part, other, mine, theirs, sensor, halo, vol, inv, kp)


def solution(mesh):
    in_specs = (
        P("depth", "parts", "band"),
        P("depth", None, None, None),
        P("depth", None),
        P("depth"),
        P("parts", "band"),
        P("parts", "band"),
    )
    return jax.shard_map(
        per_device, mesh=mesh, in_specs=in_specs, out_specs=P("depth", "parts", "band"), check_vma=False
    )
```

```python
import functools
import jax
import jax.numpy as jnp
from jax import lax
from jax.experimental import pallas as pl
from jax.experimental.pallas import tpu as pltpu
from jax.sharding import PartitionSpec as P

LX = 96
BF = jnp.bfloat16
F32 = jnp.float32
PADW = 384
SPLIT_VMEM = 24 << 20

SMEM = pl.BlockSpec(memory_space=pltpu.SMEM)
VMEM = pl.BlockSpec(memory_space=pltpu.VMEM)
ANY = pl.BlockSpec(memory_space=pl.ANY)


def dot(a, b):
    return lax.dot_general(a, b, (((1,), (0,)), ((), ())), preferred_element_type=F32)


def dot_t(a, b):
    return lax.dot_general(a, b, (((1,), (1,)), ((), ())), preferred_element_type=F32)


def count_of(info, plane):
    return info[1][plane]


def place(info, plane, slot):
    ident = info[0][plane, slot]
    start = pl.multiple_of((2 - ident // 3) * LX, LX)
    return start, jnp.where(slot < count_of(info, plane), ident % 3, 3)


def by_pairs(info, plane, slots, body):
    pairs = (count_of(info, plane) + 1) // 2
    for k in range(1, (slots + 1) // 2 + 1):
        pl.when(pairs == k)(functools.partial(body, min(2 * k, slots)))


def project_slab(info, plane, x, kp, acc):
    rows, vox = x.shape

    def body(used):
        out = dot_t(x[...], kp[plane, 0:used].reshape(used * PADW, vox))
        for s in range(used):
            row, dx = place(info, plane, s)
            acc[dx, pl.ds(row, rows), :] += out[:, s * PADW : (s + 1) * PADW]

    by_pairs(info, plane, kp.shape[1], body)


def back_slab(info, plane, ratios, kp, acc):
    lens, vox = acc.shape

    def body(used):
        left = []
        for s in range(used):
            row, dx = place(info, plane, s)
            left.append(ratios[dx, pl.ds(row, lens), :])
        acc[...] = dot(jnp.concatenate(left, axis=1), kp[plane, 0:used].reshape(used * PADW, vox))

    by_pairs(info, plane, kp.shape[1], body)


def each_plane(planes, body):
    lax.fori_loop(0, planes, lambda z, carry: (body(z), carry)[1], 0)


def column_of(rows, width):
    return lax.rem(lax.broadcasted_iota(jnp.int32, (rows, width), 0), LX)


def fold_dx(acc):
    rows = acc.shape[1]
    col = column_of(rows, PADW)
    left = jnp.where(col > 0, pltpu.roll(acc[0], 1, 0), 0.0)
    right = jnp.where(col < LX - 1, pltpu.roll(acc[2], rows - 1, 0), 0.0)
    return acc[1] + left + right


def split_kernel(psf, kp):
    slots, pix, planes, vox = psf.shape
    full = pix // 16 * 16
    kp[:, :, full:PADW, :] = jnp.zeros((planes, slots, PADW - full, vox), BF)
    for s in range(slots):
        both = jnp.swapaxes(psf[s], 0, 1)
        for z in range(planes):
            kp[z, s, 0:pix, :] = both[z]


def split_call(psf):
    planes, slots, pix, vox = psf.shape
    return pl.pallas_call(
        split_kernel,
        out_shape=jax.ShapeDtypeStruct((planes, slots, PADW, vox), BF),
        in_specs=[VMEM],
        out_specs=VMEM,
        compiler_params=pltpu.CompilerParams(vmem_limit_bytes=SPLIT_VMEM),
        cost_estimate=cost(5),
        name="split_planes",
    )(jnp.transpose(psf, (1, 2, 0, 3)))


def first_kernel(ids, counts, est, kp, part_out, send_out, est_out, xs, acc):
    acc[0:3] = jnp.zeros((3,) + acc.shape[1:], F32)

    def body(z):
        t = est[z].T
        est_out[z] = t
        xs[...] = t.astype(BF)
        project_slab((ids, counts), z, xs, kp, acc)

    each_plane(est.shape[0], body)
    keep_part(fold_dx(acc), part_out, send_out)


def first_call(estimate, kp, ids, counts):
    planes, vox, lens = estimate.shape
    rows = lens + 2 * LX
    return pl.pallas_call(
        first_kernel,
        out_shape=(
            jax.ShapeDtypeStruct((rows, PADW), F32),
            jax.ShapeDtypeStruct((2 * LX, PADW), F32),
            jax.ShapeDtypeStruct((planes, lens, vox), F32),
        ),
        in_specs=[SMEM, SMEM, VMEM, VMEM],
        out_specs=(VMEM, VMEM, VMEM),
        scratch_shapes=[
            pltpu.VMEM((lens, vox), BF),
            pltpu.VMEM((4, rows, PADW), F32),
        ],
        compiler_params=pltpu.CompilerParams(vmem_limit_bytes=36 << 20),
        cost_estimate=cost(5),
        name="project_first",
    )(ids, counts, estimate, kp)


def cost(us):
    return pl.CostEstimate(flops=int(us * 1e9), bytes_accessed=int(us * 3e6), transcendentals=0)


def upward():
    return lax.rem(lax.axis_index("band") + lax.axis_index("depth"), 2) == 1


def sensor_kernel(meas, bg, out):
    pix = meas.shape[0]
    out[...] = jnp.zeros(out.shape, F32)
    out[0, :, 0:pix] = meas[...].T
    out[1, :, 0:pix] = bg[...].T


def sensor_call(measured, background):
    lens = measured.shape[1]
    return pl.pallas_call(
        sensor_kernel,
        out_shape=jax.ShapeDtypeStruct((2, lens, PADW), F32),
        in_specs=[VMEM, VMEM],
        out_specs=VMEM,
        compiler_params=pltpu.CompilerParams(vmem_limit_bytes=16 << 20),
        cost_estimate=cost(1),
        name="sensor_turn",
    )(measured, background)


def keep_part(total, part_out, send_out):
    part_out[...] = total
    rows = part_out.shape[0]
    start = pl.multiple_of(jnp.where(upward(), 0, rows - 2 * LX), LX)
    send_out[...] = part_out[pl.ds(start, 2 * LX), :]


def edge_kernel(own, other, *refs):
    out = refs[-1]
    rows = own.shape[0]
    up = upward()
    base = pl.multiple_of(jnp.where(up, rows - 2 * LX, 0), LX)
    for i in range(2):
        line = pl.multiple_of(jnp.where(up, LX - i * LX, i * LX), LX)
        out[i] = (own[pl.ds(base + line, LX), :] + other[pl.ds(line, LX), :]).astype(BF)
    for sensor in refs[:-1]:
        line = pl.multiple_of(jnp.where(up, rows - 3 * LX, 0), LX)
        for i in range(2):
            out[2 + i] = sensor[i, pl.ds(line, LX), :].astype(BF)


def edge_call(own, other, *sensor):
    return pl.pallas_call(
        edge_kernel,
        out_shape=jax.ShapeDtypeStruct((2 + 2 * len(sensor), LX, PADW), BF),
        in_specs=[VMEM] * (2 + len(sensor)),
        out_specs=VMEM,
        compiler_params=pltpu.CompilerParams(vmem_limit_bytes=16 << 20),
        cost_estimate=cost(0.3),
        name="edge_rows",
    )(own, other, *sensor)


def ratio_planes(own, other, mine, theirs, sensor, sensor_mine, sensor_theirs, planes_ref, pix):
    rows = own.shape[0]
    lens = rows - 2 * LX
    band = lax.axis_index("band")
    up = upward()

    def both(a, b, start):
        pair = [(a[i].astype(F32), b[i].astype(F32)) for i in (start, start + 1)]
        return [jnp.where(up, x, y) for x, y in pair], [jnp.where(up, y, x) for x, y in pair]

    upper, lower = both(mine, theirs, 0)
    sensor_up, sensor_low = both(sensor_mine, sensor_theirs, 2)
    below = band > 0
    above = band < lax.axis_size("band") - 1
    lane = lax.broadcasted_iota(jnp.int32, (1, PADW), 1) < pix

    def ratio(start, size, extra, measured, background, there):
        total = own[start : start + size, :] + other[start : start + size, :]
        if extra is not None:
            total = total + extra
        keep = lane if there is None else jnp.logical_and(lane, there)
        return jnp.where(keep, measured / (total + background), 0.0).astype(BF).astype(F32)

    parts = [
        ratio(0, LX, lower[1], sensor_low[0], sensor_low[1], below),
        ratio(LX, LX, jnp.where(below, lower[0], 0.0), sensor[0, 0:LX], sensor[1, 0:LX], None),
        ratio(2 * LX, lens - 2 * LX, None, sensor[0, LX : lens - LX], sensor[1, LX : lens - LX], None),
        ratio(lens, LX, jnp.where(above, upper[0], 0.0), sensor[0, lens - LX : lens], sensor[1, lens - LX : lens], None),
        ratio(lens + LX, LX, upper[1], sensor_up[0], sensor_up[1], above),
    ]
    whole = jnp.concatenate(parts, axis=0)
    col = column_of(rows, PADW)
    planes_ref[1] = whole.astype(BF)
    planes_ref[2] = jnp.where(col > 0, pltpu.roll(whole, 1, 0), 0.0).astype(BF)
    planes_ref[0] = jnp.where(col < LX - 1, pltpu.roll(whole, rows - 1, 0), 0.0).astype(BF)
    planes_ref[3] = jnp.zeros((rows, PADW), BF)


def sensitivity_kernel(ids, counts, kp, after, inv_out):
    planes, even, _, vox = kp.shape
    lens = inv_out.shape[1]
    width = even * PADW
    lane = lax.broadcasted_iota(jnp.int32, (16, width), 1)
    slot = lax.broadcasted_iota(jnp.int32, (16, width), 0)
    ones = jnp.where(lane // PADW == slot, 1.0, 0.0).astype(BF)
    lane = lax.broadcasted_iota(jnp.int32, (1, 128), 1)
    slot = lax.rem(lane, 16)
    l = lax.broadcasted_iota(jnp.int32, (lens, 128), 0)
    grid_rows = lens // LX * lax.axis_size("band")
    row = lax.axis_index("band") * (lens // LX) + l // LX
    col = lax.rem(l, LX)

    def body(z):
        sums = dot(ones, kp[z].reshape(width, vox))
        high = sums.astype(BF).astype(F32)
        mid = (sums - high).astype(BF).astype(F32)
        low = sums - high - mid
        right = jnp.concatenate([high, mid, low, jnp.zeros((80, vox), F32)], axis=0).astype(BF)
        dy = jnp.zeros((1, 128), jnp.int32)
        dx = jnp.zeros((1, 128), jnp.int32)
        for s in range(ids.shape[1]):
            dy = jnp.where(slot == s, ids[z, s] // 3 - 1, dy)
            dx = jnp.where(slot == s, ids[z, s] % 3 - 1, dx)
        active = (slot < counts[z]) & (lane < 48)
        r = row - dy
        c = col - dx
        inside = (r >= 0) & (r < grid_rows) & (c >= 0) & (c < LX) & active
        inv_out[z] = 1.0 / dot(jnp.where(inside, 1.0, 0.0).astype(BF), right)

    each_plane(planes, body)


def sensitivity_call(ids, counts, kp, lens, after):
    planes, _, _, vox = kp.shape
    return pl.pallas_call(
        sensitivity_kernel,
        out_shape=jax.ShapeDtypeStruct((planes, lens, vox), F32),
        in_specs=[SMEM, SMEM, VMEM, ANY],
        out_specs=VMEM,
        compiler_params=pltpu.CompilerParams(vmem_limit_bytes=16 << 20),
        cost_estimate=cost(3),
        name="sensitivity",
    )(ids, counts, kp, after)


def middle_kernel(
    pix, ids, counts, own, other, mine, theirs, sensor, est, inv, kp,
    part_out, send_out, vol_out, ratios, xs, back, acc,
):
    ratio_planes(own, other, mine, theirs, sensor, mine, theirs, ratios, pix)
    acc[0:3] = jnp.zeros((3,) + acc.shape[1:], F32)

    def body(z):
        back_slab((ids, counts), z, ratios, kp, back)
        vol = est[z] * back[...] * inv[z]
        vol_out[z] = vol
        xs[...] = vol.astype(BF)
        project_slab((ids, counts), z, xs, kp, acc)

    each_plane(est.shape[0], body)
    keep_part(fold_dx(acc), part_out, send_out)


def middle_call(pix, ids, counts, own, other, mine, theirs, sensor, est, inv, kp):
    planes, lens, vox = est.shape
    rows = own.shape[0]
    return pl.pallas_call(
        functools.partial(middle_kernel, pix),
        out_shape=(
            jax.ShapeDtypeStruct((rows, PADW), F32),
            jax.ShapeDtypeStruct((2 * LX, PADW), F32),
            jax.ShapeDtypeStruct((planes, lens, vox), F32),
        ),
        in_specs=[SMEM, SMEM] + [VMEM] * 8,
        out_specs=(VMEM,) * 3,
        scratch_shapes=[
            pltpu.VMEM((4, rows, PADW), BF),
            pltpu.VMEM((lens, vox), BF),
            pltpu.VMEM((lens, vox), F32),
            pltpu.VMEM((4, rows, PADW), F32),
        ],
        compiler_params=pltpu.CompilerParams(vmem_limit_bytes=36 << 20),
        cost_estimate=cost(10),
        name="back_and_project",
    )(ids, counts, own, other, mine, theirs, sensor, est, inv, kp)


def last_kernel(
    pix, ids, counts, own, other, mine, theirs, sensor, sensor_mine, sensor_theirs, vol, inv, kp,
    out, ratios, back, turned, sem,
):
    ratio_planes(own, other, mine, theirs, sensor, sensor_mine, sensor_theirs, ratios, pix)

    def copy(z):
        return pltpu.make_async_copy(turned.at[z], out.at[z], sem.at[z])

    def body(z):
        back_slab((ids, counts), z, ratios, kp, back)
        turned[z] = (vol[z] * back[...] * inv[z]).T
        copy(z).start()

    each_plane(vol.shape[0], body)
    each_plane(vol.shape[0], lambda z: copy(z).wait())


def last_call(pix, ids, counts, own, other, mine, theirs, sensors, vol, inv, kp):
    planes, lens, vox = vol.shape
    rows = own.shape[0]
    return pl.pallas_call(
        functools.partial(last_kernel, pix),
        out_shape=jax.ShapeDtypeStruct((planes, vox, lens), F32),
        in_specs=[SMEM, SMEM] + [VMEM] * 10,
        out_specs=ANY,
        scratch_shapes=[
            pltpu.VMEM((4, rows, PADW), BF),
            pltpu.VMEM((lens, vox), F32),
            pltpu.VMEM((planes, vox, lens), F32),
            pltpu.SemaphoreType.DMA((planes,)),
        ],
        compiler_params=pltpu.CompilerParams(vmem_limit_bytes=36 << 20),
        cost_estimate=cost(6),
        name="back_last",
    )(ids, counts, own, other, mine, theirs, *sensors, vol, inv, kp)


def swap(x):
    return lax.ppermute(x, "depth", [(0, 1), (1, 0)])


def edge_exchange(x):
    parts, bands, depth = (lax.axis_size(a) for a in ("parts", "band", "depth"))
    pairs = []
    for p in range(parts):
        for b in range(bands):
            for d in range(depth):
                q, c = p, b + (1 if (b + d) % 2 == 1 else -1)
                if c < 0 or c == bands:
                    q, c = min(p ^ 1, parts - 1), b
                pairs.append(((p * bands + b) * depth + d, (q * bands + c) * depth + d))
    return lax.ppermute(x, ("parts", "band", "depth"), pairs)


def per_device(estimate, psf_blocks, offset_ids, block_counts, measured, background):
    pix, lens = measured.shape
    kp = split_call(psf_blocks)
    part, send, est = first_call(estimate, kp, offset_ids, block_counts)
    sum_edge = swap(send)
    sensor = sensor_call(measured, background)
    edges, part = lax.optimization_barrier((edge_call(part, sum_edge, sensor), part))
    mine = edge_exchange(edges)
    inv = sensitivity_call(offset_ids, block_counts, kp, lens, edges)
    other = swap(part)
    mine, inv = lax.optimization_barrier((mine, inv))
    theirs = swap(mine)
    sensors = (sensor, mine, theirs)
    part, send, vol = middle_call(
        pix, offset_ids, block_counts, part, other, mine, theirs, sensor, est, inv, kp
    )
    edges, part = lax.optimization_barrier((edge_call(part, swap(send)), part))
    mine = edge_exchange(edges)
    other = swap(part)
    return last_call(pix, offset_ids, block_counts, part, other, mine, swap(mine), sensors, vol, inv, kp)


def solution(mesh):
    in_specs = (
        P("depth", "parts", "band"),
        P("depth", None, None, None),
        P("depth", None),
        P("depth"),
        P("parts", "band"),
        P("parts", "band"),
    )
    return jax.shard_map(
        per_device, mesh=mesh, in_specs=in_specs, out_specs=P("depth", "parts", "band"), check_vma=False
    )
```

```python
import functools
import jax
import jax.numpy as jnp
from jax import lax
from jax.experimental import pallas as pl
from jax.experimental.pallas import tpu as pltpu
from jax.sharding import PartitionSpec as P

LX = 96
BF = jnp.bfloat16
F32 = jnp.float32
PADW = 384
SPLIT_VMEM = 24 << 20

SMEM = pl.BlockSpec(memory_space=pltpu.SMEM)
VMEM = pl.BlockSpec(memory_space=pltpu.VMEM)
ANY = pl.BlockSpec(memory_space=pl.ANY)


def dot(a, b):
    return lax.dot_general(a, b, (((1,), (0,)), ((), ())), preferred_element_type=F32)


def dot_t(a, b):
    return lax.dot_general(a, b, (((1,), (1,)), ((), ())), preferred_element_type=F32)


def count_of(info, plane):
    return info[1][plane]


def place(info, plane, slot):
    ident = info[0][plane, slot]
    start = pl.multiple_of((2 - ident // 3) * LX, LX)
    return start, jnp.where(slot < count_of(info, plane), ident % 3, 3)


def by_pairs(info, plane, slots, body):
    pairs = (count_of(info, plane) + 1) // 2
    for k in range(1, (slots + 1) // 2 + 1):
        pl.when(pairs == k)(functools.partial(body, min(2 * k, slots)))


def project_slab(info, plane, x, kp, acc):
    rows, vox = x.shape

    def body(used):
        out = dot_t(x[...], kp[plane, 0:used].reshape(used * PADW, vox))
        for s in range(used):
            row, dx = place(info, plane, s)
            acc[dx, pl.ds(row, rows), :] += out[:, s * PADW : (s + 1) * PADW]

    by_pairs(info, plane, kp.shape[1], body)


def back_slab(info, plane, ratios, kp, acc):
    lens, vox = acc.shape

    def body(used):
        left = []
        for s in range(used):
            row, dx = place(info, plane, s)
            left.append(ratios[dx, pl.ds(row, lens), :])
        acc[...] = dot(jnp.concatenate(left, axis=1), kp[plane, 0:used].reshape(used * PADW, vox))

    by_pairs(info, plane, kp.shape[1], body)


def each_plane(planes, body):
    lax.fori_loop(0, planes, lambda z, carry: (body(z), carry)[1], 0)


def column_of(rows, width):
    return lax.rem(lax.broadcasted_iota(jnp.int32, (rows, width), 0), LX)


def fold_dx(acc):
    rows = acc.shape[1]
    col = column_of(rows, PADW)
    left = jnp.where(col > 0, pltpu.roll(acc[0], 1, 0), 0.0)
    right = jnp.where(col < LX - 1, pltpu.roll(acc[2], rows - 1, 0), 0.0)
    return acc[1] + left + right


def split_kernel(psf, after, kp):
    slots, pix, planes, vox = psf.shape
    full = pix // 16 * 16
    kp[:, :, full:PADW, :] = jnp.zeros((planes, slots, PADW - full, vox), BF)
    for s in range(slots):
        both = jnp.swapaxes(psf[s], 0, 1)
        for z in range(planes):
            kp[z, s, 0:pix, :] = both[z]


def split_call(psf, after):
    planes, slots, pix, vox = psf.shape
    return pl.pallas_call(
        split_kernel,
        out_shape=jax.ShapeDtypeStruct((planes, slots, PADW, vox), BF),
        in_specs=[VMEM, ANY],
        out_specs=VMEM,
        compiler_params=pltpu.CompilerParams(vmem_limit_bytes=SPLIT_VMEM),
        cost_estimate=cost(5),
        name="split_planes",
    )(jnp.transpose(psf, (1, 2, 0, 3)), after)


def first_kernel(ids, counts, est, kp, part_out, send_out, est_out, xs, acc):
    acc[0:3] = jnp.zeros((3,) + acc.shape[1:], F32)

    def body(z):
        t = est[z].T
        est_out[z] = t
        xs[...] = t.astype(BF)
        project_slab((ids, counts), z, xs, kp, acc)

    each_plane(est.shape[0], body)
    keep_part(fold_dx(acc), part_out, send_out)


def first_call(estimate, kp, ids, counts):
    planes, vox, lens = estimate.shape
    rows = lens + 2 * LX
    return pl.pallas_call(
        first_kernel,
        out_shape=(
            jax.ShapeDtypeStruct((rows, PADW), F32),
            jax.ShapeDtypeStruct((2 * LX, PADW), F32),
            jax.ShapeDtypeStruct((planes, lens, vox), F32),
        ),
        in_specs=[SMEM, SMEM, VMEM, VMEM],
        out_specs=(VMEM, VMEM, VMEM),
        scratch_shapes=[
            pltpu.VMEM((lens, vox), BF),
            pltpu.VMEM((4, rows, PADW), F32),
        ],
        compiler_params=pltpu.CompilerParams(vmem_limit_bytes=36 << 20),
        cost_estimate=cost(5),
        name="project_first",
    )(ids, counts, estimate, kp)


def cost(us):
    return pl.CostEstimate(flops=int(us * 1e9), bytes_accessed=int(us * 3e6), transcendentals=0)


def upward():
    return lax.rem(lax.axis_index("band") + lax.axis_index("depth"), 2) == 1


def sensor_kernel(meas, bg, out, edge):
    pix, lens = meas.shape
    out[...] = jnp.zeros(out.shape, F32)
    out[0, :, 0:pix] = meas[...].T
    out[1, :, 0:pix] = bg[...].T
    line = pl.multiple_of(jnp.where(upward(), lens - LX, 0), LX)
    edge[:, 0:LX] = out[:, pl.ds(line, LX), :]
    edge[:, LX:] = jnp.zeros((2, edge.shape[1] - LX, PADW), F32)


def sensor_call(measured, background):
    lens = measured.shape[1]
    return pl.pallas_call(
        sensor_kernel,
        out_shape=(
            jax.ShapeDtypeStruct((2, lens, PADW), F32),
            jax.ShapeDtypeStruct((2, LX + 8, PADW), F32),
        ),
        in_specs=[VMEM, VMEM],
        out_specs=(VMEM, VMEM),
        compiler_params=pltpu.CompilerParams(vmem_limit_bytes=16 << 20),
        cost_estimate=cost(8),
        name="sensor_turn",
    )(measured, background)


def keep_part(total, part_out, send_out):
    part_out[...] = total
    rows = part_out.shape[0]
    start = pl.multiple_of(jnp.where(upward(), 0, rows - 2 * LX), LX)
    send_out[...] = part_out[pl.ds(start, 2 * LX), :]


def edge_kernel(own, other, out):
    rows = own.shape[0]
    up = upward()
    base = pl.multiple_of(jnp.where(up, rows - 2 * LX, 0), LX)
    for i in range(2):
        line = pl.multiple_of(jnp.where(up, LX - i * LX, i * LX), LX)
        out[i] = (own[pl.ds(base + line, LX), :] + other[pl.ds(line, LX), :]).astype(BF)


def edge_call(own, other):
    return pl.pallas_call(
        edge_kernel,
        out_shape=jax.ShapeDtypeStruct((2, LX, PADW), BF),
        in_specs=[VMEM, VMEM],
        out_specs=VMEM,
        compiler_params=pltpu.CompilerParams(vmem_limit_bytes=16 << 20),
        cost_estimate=cost(0.3),
        name="edge_rows",
    )(own, other)


def ratio_planes(own, other, mine, theirs, sensor, sensor_mine, sensor_theirs, planes_ref, pix):
    rows = own.shape[0]
    lens = rows - 2 * LX
    band = lax.axis_index("band")
    up = upward()

    def both(a, b):
        pair = [(a[i, 0:LX].astype(F32), b[i, 0:LX].astype(F32)) for i in range(2)]
        return [jnp.where(up, x, y) for x, y in pair], [jnp.where(up, y, x) for x, y in pair]

    upper, lower = both(mine, theirs)
    sensor_up, sensor_low = both(sensor_mine, sensor_theirs)
    below = band > 0
    above = band < lax.axis_size("band") - 1
    lane = lax.broadcasted_iota(jnp.int32, (1, PADW), 1) < pix

    def ratio(start, size, extra, measured, background, there):
        total = own[start : start + size, :] + other[start : start + size, :]
        if extra is not None:
            total = total + extra
        keep = lane if there is None else jnp.logical_and(lane, there)
        return jnp.where(keep, measured / (total + background), 0.0).astype(BF).astype(F32)

    parts = [
        ratio(0, LX, lower[1], sensor_low[0], sensor_low[1], below),
        ratio(LX, LX, jnp.where(below, lower[0], 0.0), sensor[0, 0:LX], sensor[1, 0:LX], None),
        ratio(2 * LX, lens - 2 * LX, None, sensor[0, LX : lens - LX], sensor[1, LX : lens - LX], None),
        ratio(lens, LX, jnp.where(above, upper[0], 0.0), sensor[0, lens - LX : lens], sensor[1, lens - LX : lens], None),
        ratio(lens + LX, LX, upper[1], sensor_up[0], sensor_up[1], above),
    ]
    whole = jnp.concatenate(parts, axis=0)
    col = column_of(rows, PADW)
    planes_ref[1] = whole.astype(BF)
    planes_ref[2] = jnp.where(col > 0, pltpu.roll(whole, 1, 0), 0.0).astype(BF)
    planes_ref[0] = jnp.where(col < LX - 1, pltpu.roll(whole, rows - 1, 0), 0.0).astype(BF)
    planes_ref[3] = jnp.zeros((rows, PADW), BF)


def sensitivity_kernel(ids, counts, kp, after, inv_out):
    planes, even, _, vox = kp.shape
    lens = inv_out.shape[1]
    width = even * PADW
    lane = lax.broadcasted_iota(jnp.int32, (16, width), 1)
    slot = lax.broadcasted_iota(jnp.int32, (16, width), 0)
    ones = jnp.where(lane // PADW == slot, 1.0, 0.0).astype(BF)
    lane = lax.broadcasted_iota(jnp.int32, (1, 128), 1)
    slot = lax.rem(lane, 16)
    l = lax.broadcasted_iota(jnp.int32, (lens, 128), 0)
    grid_rows = lens // LX * lax.axis_size("band")
    row = lax.axis_index("band") * (lens // LX) + l // LX
    col = lax.rem(l, LX)

    def body(z):
        sums = dot(ones, kp[z].reshape(width, vox))
        high = sums.astype(BF).astype(F32)
        mid = (sums - high).astype(BF).astype(F32)
        low = sums - high - mid
        right = jnp.concatenate([high, mid, low, jnp.zeros((80, vox), F32)], axis=0).astype(BF)
        dy = jnp.zeros((1, 128), jnp.int32)
        dx = jnp.zeros((1, 128), jnp.int32)
        for s in range(ids.shape[1]):
            dy = jnp.where(slot == s, ids[z, s] // 3 - 1, dy)
            dx = jnp.where(slot == s, ids[z, s] % 3 - 1, dx)
        active = (slot < counts[z]) & (lane < 48)
        r = row - dy
        c = col - dx
        inside = (r >= 0) & (r < grid_rows) & (c >= 0) & (c < LX) & active
        inv_out[z] = 1.0 / dot(jnp.where(inside, 1.0, 0.0).astype(BF), right)

    each_plane(planes, body)


def sensitivity_call(ids, counts, kp, lens, after):
    planes, _, _, vox = kp.shape
    return pl.pallas_call(
        sensitivity_kernel,
        out_shape=jax.ShapeDtypeStruct((planes, lens, vox), F32),
        in_specs=[SMEM, SMEM, VMEM, ANY],
        out_specs=VMEM,
        compiler_params=pltpu.CompilerParams(vmem_limit_bytes=16 << 20),
        cost_estimate=cost(3),
        name="sensitivity",
    )(ids, counts, kp, after)


def middle_kernel(
    pix, ids, counts, own, other, mine, theirs, sensor, sensor_mine, sensor_theirs, est, inv, kp,
    part_out, send_out, vol_out, ratios, xs, back, acc,
):
    ratio_planes(own, other, mine, theirs, sensor, sensor_mine, sensor_theirs, ratios, pix)
    acc[0:3] = jnp.zeros((3,) + acc.shape[1:], F32)

    def body(z):
        back_slab((ids, counts), z, ratios, kp, back)
        vol = est[z] * back[...] * inv[z]
        vol_out[z] = vol
        xs[...] = vol.astype(BF)
        project_slab((ids, counts), z, xs, kp, acc)

    each_plane(est.shape[0], body)
    keep_part(fold_dx(acc), part_out, send_out)


def middle_call(pix, ids, counts, own, other, mine, theirs, sensors, est, inv, kp):
    planes, lens, vox = est.shape
    rows = own.shape[0]
    return pl.pallas_call(
        functools.partial(middle_kernel, pix),
        out_shape=(
            jax.ShapeDtypeStruct((rows, PADW), F32),
            jax.ShapeDtypeStruct((2 * LX, PADW), F32),
            jax.ShapeDtypeStruct((planes, lens, vox), F32),
        ),
        in_specs=[SMEM, SMEM] + [VMEM] * 10,
        out_specs=(VMEM,) * 3,
        scratch_shapes=[
            pltpu.VMEM((4, rows, PADW), BF),
            pltpu.VMEM((lens, vox), BF),
            pltpu.VMEM((lens, vox), F32),
            pltpu.VMEM((4, rows, PADW), F32),
        ],
        compiler_params=pltpu.CompilerParams(vmem_limit_bytes=36 << 20),
        cost_estimate=cost(10),
        name="back_and_project",
    )(ids, counts, own, other, mine, theirs, *sensors, est, inv, kp)


def last_kernel(
    pix, ids, counts, own, other, mine, theirs, sensor, sensor_mine, sensor_theirs, vol, inv, kp,
    out, ratios, back, turned, sem,
):
    ratio_planes(own, other, mine, theirs, sensor, sensor_mine, sensor_theirs, ratios, pix)

    def copy(z):
        return pltpu.make_async_copy(turned.at[z], out.at[z], sem.at[z])

    def body(z):
        back_slab((ids, counts), z, ratios, kp, back)
        turned[z] = (vol[z] * back[...] * inv[z]).T
        copy(z).start()

    each_plane(vol.shape[0], body)
    each_plane(vol.shape[0], lambda z: copy(z).wait())


def last_call(pix, ids, counts, own, other, mine, theirs, sensors, vol, inv, kp):
    planes, lens, vox = vol.shape
    rows = own.shape[0]
    return pl.pallas_call(
        functools.partial(last_kernel, pix),
        out_shape=jax.ShapeDtypeStruct((planes, vox, lens), F32),
        in_specs=[SMEM, SMEM] + [VMEM] * 10,
        out_specs=ANY,
        scratch_shapes=[
            pltpu.VMEM((4, rows, PADW), BF),
            pltpu.VMEM((lens, vox), F32),
            pltpu.VMEM((planes, vox, lens), F32),
            pltpu.SemaphoreType.DMA((planes,)),
        ],
        compiler_params=pltpu.CompilerParams(vmem_limit_bytes=36 << 20),
        cost_estimate=cost(6),
        name="back_last",
    )(ids, counts, own, other, mine, theirs, *sensors, vol, inv, kp)


def swap(x):
    return lax.ppermute(x, "depth", [(0, 1), (1, 0)])


def edge_exchange(x):
    parts, bands, depth = (lax.axis_size(a) for a in ("parts", "band", "depth"))
    pairs = []
    for p in range(parts):
        for b in range(bands):
            for d in range(depth):
                q, c = p, b + (1 if (b + d) % 2 == 1 else -1)
                if c < 0 or c == bands:
                    q, c = min(p ^ 1, parts - 1), b
                pairs.append(((p * bands + b) * depth + d, (q * bands + c) * depth + d))
    return lax.ppermute(x, ("parts", "band", "depth"), pairs)


def per_device(estimate, psf_blocks, offset_ids, block_counts, measured, background):
    pix, lens = measured.shape
    sensor, sensor_edge = sensor_call(measured, background)
    sensor_mine = edge_exchange(sensor_edge)
    kp = split_call(psf_blocks, sensor_edge)
    part, send, est = first_call(estimate, kp, offset_ids, block_counts)
    sum_edge, sensor_mine = lax.optimization_barrier((swap(send), sensor_mine))
    edges, part = lax.optimization_barrier((edge_call(part, sum_edge), part))
    mine = edge_exchange(edges)
    inv = sensitivity_call(offset_ids, block_counts, kp, lens, edges)
    other = swap(part)
    sensors = (sensor, sensor_mine, swap(sensor_mine))
    mine, inv = lax.optimization_barrier((mine, inv))
    part, send, vol = middle_call(
        pix, offset_ids, block_counts, part, other, mine, swap(mine), sensors, est, inv, kp
    )
    edges, part = lax.optimization_barrier((edge_call(part, swap(send)), part))
    mine = edge_exchange(edges)
    other = swap(part)
    return last_call(pix, offset_ids, block_counts, part, other, mine, swap(mine), sensors, vol, inv, kp)


def solution(mesh):
    in_specs = (
        P("depth", "parts", "band"),
        P("depth", None, None, None),
        P("depth", None),
        P("depth"),
        P("parts", "band"),
        P("parts", "band"),
    )
    return jax.shard_map(
        per_device, mesh=mesh, in_specs=in_specs, out_specs=P("depth", "parts", "band"), check_vma=False
    )
```

```python
import functools
import jax
import jax.numpy as jnp
from jax import lax
from jax.experimental import pallas as pl
from jax.experimental.pallas import tpu as pltpu
from jax.sharding import PartitionSpec as P

LX = 96
BF = jnp.bfloat16
F32 = jnp.float32
PADW = 384
SPLIT_VMEM = 24 << 20

SMEM = pl.BlockSpec(memory_space=pltpu.SMEM)
VMEM = pl.BlockSpec(memory_space=pltpu.VMEM)
ANY = pl.BlockSpec(memory_space=pl.ANY)


def dot(a, b):
    return lax.dot_general(a, b, (((1,), (0,)), ((), ())), preferred_element_type=F32)


def dot_t(a, b):
    return lax.dot_general(a, b, (((1,), (1,)), ((), ())), preferred_element_type=F32)


def fetch(ids_in, counts_in, ids, counts, sem):
    copies = [
        pltpu.make_async_copy(ids_in, ids, sem.at[0]),
        pltpu.make_async_copy(counts_in, counts, sem.at[1]),
    ]
    for c in copies:
        c.start()
    return copies


def list_scratch(ids, counts):
    return [pltpu.SMEM(ids.shape, ids.dtype), pltpu.SMEM(counts.shape, counts.dtype), pltpu.SemaphoreType.DMA((2,))]


def count_of(info, plane):
    return info[1][plane]


def place(info, plane, slot):
    ident = info[0][plane, slot]
    start = pl.multiple_of((2 - ident // 3) * LX, LX)
    return start, jnp.where(slot < count_of(info, plane), ident % 3, 3)


def by_pairs(info, plane, slots, body):
    pairs = (count_of(info, plane) + 1) // 2
    for k in range(1, (slots + 1) // 2 + 1):
        pl.when(pairs == k)(functools.partial(body, min(2 * k, slots)))


def project_slab(info, plane, x, kp, acc):
    rows, vox = x.shape

    def body(used):
        out = dot_t(x[...], kp[plane, 0:used].reshape(used * PADW, vox))
        for s in range(used):
            row, dx = place(info, plane, s)
            acc[dx, pl.ds(row, rows), :] += out[:, s * PADW : (s + 1) * PADW]

    by_pairs(info, plane, kp.shape[1], body)


def back_slab(info, plane, ratios, kp, lens, finish):
    vox = kp.shape[3]

    def body(used):
        left = []
        for s in range(used):
            row, dx = place(info, plane, s)
            left.append(ratios[dx, pl.ds(row, lens), :])
        finish(dot(jnp.concatenate(left, axis=1), kp[plane, 0:used].reshape(used * PADW, vox)))

    by_pairs(info, plane, kp.shape[1], body)


def each_plane(planes, body):
    lax.fori_loop(0, planes, lambda z, carry: (body(z), carry)[1], 0)


def column_of(rows, width):
    return lax.rem(lax.broadcasted_iota(jnp.int32, (rows, width), 0), LX)


def fold_dx(acc):
    rows = acc.shape[1]
    col = column_of(rows, PADW)
    left = jnp.where(col > 0, pltpu.roll(acc[0], 1, 0), 0.0)
    right = jnp.where(col < LX - 1, pltpu.roll(acc[2], rows - 1, 0), 0.0)
    return acc[1] + left + right


def split_kernel(psf, after, kp):
    slots, pix, planes, vox = psf.shape
    full = pix // 16 * 16
    kp[:, :, full:PADW, :] = jnp.zeros((planes, slots, PADW - full, vox), BF)
    for s in range(slots):
        both = jnp.swapaxes(psf[s], 0, 1)
        for z in range(planes):
            kp[z, s, 0:pix, :] = both[z]


def split_call(psf, after):
    planes, slots, pix, vox = psf.shape
    return pl.pallas_call(
        split_kernel,
        out_shape=jax.ShapeDtypeStruct((planes, slots, PADW, vox), BF),
        in_specs=[VMEM, ANY],
        out_specs=VMEM,
        compiler_params=pltpu.CompilerParams(vmem_limit_bytes=SPLIT_VMEM),
        cost_estimate=cost(5),
        name="split_planes",
    )(jnp.transpose(psf, (1, 2, 0, 3)), after)


def first_kernel(ids_in, counts_in, est, kp, part_out, send_out, est_out, xs, acc, ids, counts, sem):
    copies = fetch(ids_in, counts_in, ids, counts, sem)
    acc[0:3] = jnp.zeros((3,) + acc.shape[1:], F32)

    def body(z):
        t = est[z].T
        est_out[z] = t
        xs[...] = t.astype(BF)
        project_slab((ids, counts), z, xs, kp, acc)

    for c in copies:
        c.wait()
    each_plane(est.shape[0], body)
    keep_part(fold_dx(acc), part_out, send_out)


def first_call(estimate, kp, ids, counts):
    planes, vox, lens = estimate.shape
    rows = lens + 2 * LX
    return pl.pallas_call(
        first_kernel,
        out_shape=(
            jax.ShapeDtypeStruct((rows, PADW), F32),
            jax.ShapeDtypeStruct((2 * LX, PADW), BF),
            jax.ShapeDtypeStruct((planes, lens, vox), F32),
        ),
        in_specs=[ANY, ANY, VMEM, VMEM],
        out_specs=(VMEM, VMEM, VMEM),
        scratch_shapes=[
            pltpu.VMEM((lens, vox), BF),
            pltpu.VMEM((4, rows, PADW), F32),
        ]
        + list_scratch(ids, counts),
        compiler_params=pltpu.CompilerParams(vmem_limit_bytes=36 << 20),
        cost_estimate=cost(5),
        name="project_first",
    )(ids, counts, estimate, kp)


def cost(us):
    return pl.CostEstimate(flops=int(us * 1e9), bytes_accessed=int(us * 3e6), transcendentals=0)


def upward():
    return lax.rem(lax.axis_index("band") + lax.axis_index("depth"), 2) == 1


def sensor_kernel(meas, bg, out, edge):
    pix, lens = meas.shape
    out[...] = jnp.zeros(out.shape, F32)
    out[0, :, 0:pix] = meas[...].T
    out[1, :, 0:pix] = bg[...].T
    line = pl.multiple_of(jnp.where(upward(), lens - LX, 0), LX)
    edge[:, 0:LX] = out[:, pl.ds(line, LX), :]
    edge[:, LX:] = jnp.zeros((2, edge.shape[1] - LX, PADW), F32)


def sensor_call(measured, background):
    lens = measured.shape[1]
    return pl.pallas_call(
        sensor_kernel,
        out_shape=(
            jax.ShapeDtypeStruct((2, lens, PADW), F32),
            jax.ShapeDtypeStruct((2, LX + 8, PADW), F32),
        ),
        in_specs=[VMEM, VMEM],
        out_specs=(VMEM, VMEM),
        compiler_params=pltpu.CompilerParams(vmem_limit_bytes=16 << 20),
        cost_estimate=cost(8),
        name="sensor_turn",
    )(measured, background)


def keep_part(total, part_out, send_out):
    part_out[...] = total
    rows = part_out.shape[0]
    start = pl.multiple_of(jnp.where(upward(), 0, rows - 2 * LX), LX)
    send_out[...] = part_out[pl.ds(start, 2 * LX), :].astype(BF)


def edge_kernel(own, other, out):
    rows = own.shape[0]
    up = upward()
    base = pl.multiple_of(jnp.where(up, rows - 2 * LX, 0), LX)
    for i in range(2):
        line = pl.multiple_of(jnp.where(up, LX - i * LX, i * LX), LX)
        out[i] = (own[pl.ds(base + line, LX), :] + other[pl.ds(line, LX), :].astype(F32)).astype(BF)


def edge_call(own, other):
    return pl.pallas_call(
        edge_kernel,
        out_shape=jax.ShapeDtypeStruct((2, LX, PADW), BF),
        in_specs=[VMEM, VMEM],
        out_specs=VMEM,
        compiler_params=pltpu.CompilerParams(vmem_limit_bytes=16 << 20),
        cost_estimate=cost(0.3),
        name="edge_rows",
    )(own, other)


def ratio_rows(own, other, start, size, extra, measured, background, keep):
    total = own[start : start + size, :] + other[start : start + size, :]
    if extra is not None:
        total = total + extra
    return jnp.where(keep, measured / (total + background), 0.0).astype(BF).astype(F32)


def spread(planes_ref, start, whole):
    rows = whole.shape[0]
    col = column_of(rows, PADW)
    here = pl.ds(start, rows)
    planes_ref[1, here, :] = whole.astype(BF)
    planes_ref[2, here, :] = jnp.where(col > 0, pltpu.roll(whole, 1, 0), 0.0).astype(BF)
    planes_ref[0, here, :] = jnp.where(col < LX - 1, pltpu.roll(whole, rows - 1, 0), 0.0).astype(BF)


def real_lanes(pix):
    return lax.broadcasted_iota(jnp.int32, (1, PADW), 1) < pix


def inner_kernel(pix, own, other, sensor, out):
    size = out.shape[1]
    measured, background = (sensor[i, LX : LX + size] for i in range(2))
    spread(out, 0, ratio_rows(own, other, 2 * LX, size, None, measured, background, real_lanes(pix)))


def inner_call(pix, own, other, sensor):
    return pl.pallas_call(
        functools.partial(inner_kernel, pix),
        out_shape=jax.ShapeDtypeStruct((3, own.shape[0] - 4 * LX, PADW), BF),
        in_specs=[VMEM] * 3,
        out_specs=VMEM,
        compiler_params=pltpu.CompilerParams(vmem_limit_bytes=16 << 20),
        cost_estimate=cost(1),
        name="inner_ratio",
    )(own, other, sensor)


def ratio_planes(own, other, mine, theirs, inner, sensor, sensor_mine, sensor_theirs, planes_ref, pix):
    rows = own.shape[0]
    lens = rows - 2 * LX
    band = lax.axis_index("band")
    up = upward()

    def both(a, b):
        pair = [(a[i, 0:LX].astype(F32), b[i, 0:LX].astype(F32)) for i in range(2)]
        return [jnp.where(up, x, y) for x, y in pair], [jnp.where(up, y, x) for x, y in pair]

    upper, lower = both(mine, theirs)
    sensor_up, sensor_low = both(sensor_mine, sensor_theirs)
    below = band > 0
    above = band < lax.axis_size("band") - 1
    lane = real_lanes(pix)

    def ratio(start, extra, measured, background, keep):
        return ratio_rows(own, other, start, LX, extra, measured, background, keep)

    planes_ref[0:3, 2 * LX : lens, :] = inner[...]
    planes_ref[3] = jnp.zeros((rows, PADW), BF)
    low = [
        ratio(0, lower[1], sensor_low[0], sensor_low[1], lane & below),
        ratio(LX, jnp.where(below, lower[0], 0.0), sensor[0, 0:LX], sensor[1, 0:LX], lane),
    ]
    spread(planes_ref, 0, jnp.concatenate(low, axis=0))
    high = [
        ratio(lens, jnp.where(above, upper[0], 0.0), sensor[0, lens - LX :], sensor[1, lens - LX :], lane),
        ratio(lens + LX, upper[1], sensor_up[0], sensor_up[1], lane & above),
    ]
    spread(planes_ref, lens, jnp.concatenate(high, axis=0))


def sensitivity_kernel(ids, counts, kp, after, inv_out):
    planes, even, _, vox = kp.shape
    lens = inv_out.shape[1]
    width = even * PADW
    lane = lax.broadcasted_iota(jnp.int32, (16, width), 1)
    slot = lax.broadcasted_iota(jnp.int32, (16, width), 0)
    ones = jnp.where(lane // PADW == slot, 1.0, 0.0).astype(BF)
    lane = lax.broadcasted_iota(jnp.int32, (1, 128), 1)
    slot = lax.rem(lane, 16)
    l = lax.broadcasted_iota(jnp.int32, (lens, 128), 0)
    grid_rows = lens // LX * lax.axis_size("band")
    row = lax.axis_index("band") * (lens // LX) + l // LX
    col = lax.rem(l, LX)

    def body(z):
        sums = dot(ones, kp[z].reshape(width, vox))
        high = sums.astype(BF).astype(F32)
        mid = (sums - high).astype(BF).astype(F32)
        low = sums - high - mid
        right = jnp.concatenate([high, mid, low, jnp.zeros((80, vox), F32)], axis=0).astype(BF)
        dy = jnp.zeros((1, 128), jnp.int32)
        dx = jnp.zeros((1, 128), jnp.int32)
        for s in range(ids.shape[1]):
            dy = jnp.where(slot == s, ids[z, s] // 3 - 1, dy)
            dx = jnp.where(slot == s, ids[z, s] % 3 - 1, dx)
        active = (slot < counts[z]) & (lane < 48)
        r = row - dy
        c = col - dx
        inside = (r >= 0) & (r < grid_rows) & (c >= 0) & (c < LX) & active
        inv_out[z] = 1.0 / dot(jnp.where(inside, 1.0, 0.0).astype(BF), right)

    each_plane(planes, body)


def sensitivity_call(ids, counts, kp, lens, after):
    planes, _, _, vox = kp.shape
    return pl.pallas_call(
        sensitivity_kernel,
        out_shape=jax.ShapeDtypeStruct((planes, lens, vox), F32),
        in_specs=[SMEM, SMEM, VMEM, ANY],
        out_specs=VMEM,
        compiler_params=pltpu.CompilerParams(vmem_limit_bytes=16 << 20),
        cost_estimate=cost(3),
        name="sensitivity",
    )(ids, counts, kp, after)


def middle_kernel(
    pix, ids_in, counts_in, own, other, mine, theirs, inner, sensor, sensor_mine, sensor_theirs, est, inv, kp,
    part_out, send_out, vol_out, ratios, xs, acc, ids, counts, sem,
):
    copies = fetch(ids_in, counts_in, ids, counts, sem)
    ratio_planes(own, other, mine, theirs, inner, sensor, sensor_mine, sensor_theirs, ratios, pix)
    acc[0:3] = jnp.zeros((3,) + acc.shape[1:], F32)

    def body(z):
        def finish(back):
            vol = est[z] * back * inv[z]
            vol_out[z] = vol
            xs[...] = vol.astype(BF)

        back_slab((ids, counts), z, ratios, kp, est.shape[1], finish)
        project_slab((ids, counts), z, xs, kp, acc)

    for c in copies:
        c.wait()
    each_plane(est.shape[0], body)
    keep_part(fold_dx(acc), part_out, send_out)


def middle_call(pix, ids, counts, own, other, mine, theirs, inner, sensors, est, inv, kp):
    planes, lens, vox = est.shape
    rows = own.shape[0]
    return pl.pallas_call(
        functools.partial(middle_kernel, pix),
        out_shape=(
            jax.ShapeDtypeStruct((rows, PADW), F32),
            jax.ShapeDtypeStruct((2 * LX, PADW), BF),
            jax.ShapeDtypeStruct((planes, lens, vox), F32),
        ),
        in_specs=[ANY, ANY] + [VMEM] * 11,
        out_specs=(VMEM,) * 3,
        scratch_shapes=[
            pltpu.VMEM((4, rows, PADW), BF),
            pltpu.VMEM((lens, vox), BF),
            pltpu.VMEM((4, rows, PADW), F32),
        ]
        + list_scratch(ids, counts),
        compiler_params=pltpu.CompilerParams(vmem_limit_bytes=36 << 20),
        cost_estimate=cost(10),
        name="back_and_project",
    )(ids, counts, own, other, mine, theirs, inner, *sensors, est, inv, kp)


def last_kernel(
    pix, ids_in, counts_in, own, other, mine, theirs, inner, sensor, sensor_mine, sensor_theirs, vol, inv, kp,
    out, ratios, turned, sem, ids, counts, list_sem,
):
    copies = fetch(ids_in, counts_in, ids, counts, list_sem)
    ratio_planes(own, other, mine, theirs, inner, sensor, sensor_mine, sensor_theirs, ratios, pix)

    vox = vol.shape[2]

    def copy(z, v):
        here = pl.ds(v * 128, 128)
        return pltpu.make_async_copy(turned.at[z, here], out.at[z, here], sem.at[z, v])

    def body(z):
        def finish(back):
            for v in range(vox // 128):
                here = slice(v * 128, (v + 1) * 128)
                turned[z, here, :] = (vol[z, :, here] * back[:, here] * inv[z, :, here]).T
                copy(z, v).start()

        back_slab((ids, counts), z, ratios, kp, vol.shape[1], finish)

    for c in copies:
        c.wait()
    each_plane(vol.shape[0], body)
    for z in range(vol.shape[0]):
        for v in range(vox // 128):
            copy(z, v).wait()


def last_call(pix, ids, counts, own, other, mine, theirs, inner, sensors, vol, inv, kp):
    planes, lens, vox = vol.shape
    rows = own.shape[0]
    return pl.pallas_call(
        functools.partial(last_kernel, pix),
        out_shape=jax.ShapeDtypeStruct((planes, vox, lens), F32),
        in_specs=[ANY, ANY] + [VMEM] * 11,
        out_specs=ANY,
        scratch_shapes=[
            pltpu.VMEM((4, rows, PADW), BF),
            pltpu.VMEM((planes, vox, lens), F32),
            pltpu.SemaphoreType.DMA((planes, vox // 128)),
        ]
        + list_scratch(ids, counts),
        compiler_params=pltpu.CompilerParams(vmem_limit_bytes=36 << 20),
        cost_estimate=cost(6),
        name="back_last",
    )(ids, counts, own, other, mine, theirs, inner, *sensors, vol, inv, kp)


def swap(x):
    return lax.ppermute(x, "depth", [(0, 1), (1, 0)])


def edge_exchange(x):
    parts, bands, depth = (lax.axis_size(a) for a in ("parts", "band", "depth"))
    pairs = []
    for p in range(parts):
        for b in range(bands):
            for d in range(depth):
                q, c = p, b + (1 if (b + d) % 2 == 1 else -1)
                if c < 0 or c == bands:
                    q, c = min(p ^ 1, parts - 1), b
                pairs.append(((p * bands + b) * depth + d, (q * bands + c) * depth + d))
    return lax.ppermute(x, ("parts", "band", "depth"), pairs)


def per_device(estimate, psf_blocks, offset_ids, block_counts, measured, background):
    pix, lens = measured.shape
    sensor, sensor_edge = sensor_call(measured, background)
    sensor_mine = edge_exchange(sensor_edge)
    kp = split_call(psf_blocks, sensor_edge)
    part, send, est = first_call(estimate, kp, offset_ids, block_counts)
    sum_edge, sensor_mine = lax.optimization_barrier((swap(send), sensor_mine))
    edges, part = lax.optimization_barrier((edge_call(part, sum_edge), part))
    mine = edge_exchange(edges)
    inv = sensitivity_call(offset_ids, block_counts, kp, lens, edges)
    other = swap(part)
    sensors = (sensor, sensor_mine, swap(sensor_mine))
    inner = inner_call(pix, part, other, sensor)
    mine, inv, inner = lax.optimization_barrier((mine, inv, inner))
    part, send, vol = middle_call(
        pix, offset_ids, block_counts, part, other, mine, swap(mine), inner, sensors, est, inv, kp
    )
    edges, part = lax.optimization_barrier((edge_call(part, swap(send)), part))
    mine = edge_exchange(edges)
    other = swap(part)
    inner = inner_call(pix, part, other, sensor)
    mine, inner = lax.optimization_barrier((mine, inner))
    return last_call(pix, offset_ids, block_counts, part, other, mine, swap(mine), inner, sensors, vol, inv, kp)


def solution(mesh):
    in_specs = (
        P("depth", "parts", "band"),
        P("depth", None, None, None),
        P("depth", None),
        P("depth"),
        P("parts", "band"),
        P("parts", "band"),
    )
    return jax.shard_map(
        per_device, mesh=mesh, in_specs=in_specs, out_specs=P("depth", "parts", "band"), check_vma=False
    )
```

```python
import functools
import jax
import jax.numpy as jnp
from jax import lax
from jax.experimental import pallas as pl
from jax.experimental.pallas import tpu as pltpu
from jax.sharding import PartitionSpec as P

LX = 96
BF = jnp.bfloat16
F32 = jnp.float32
PADW = 384
SPLIT_VMEM = 24 << 20

SMEM = pl.BlockSpec(memory_space=pltpu.SMEM)
VMEM = pl.BlockSpec(memory_space=pltpu.VMEM)
ANY = pl.BlockSpec(memory_space=pl.ANY)


def dot(a, b):
    return lax.dot_general(a, b, (((1,), (0,)), ((), ())), preferred_element_type=F32)


def dot_t(a, b):
    return lax.dot_general(a, b, (((1,), (1,)), ((), ())), preferred_element_type=F32)


def fetch(ids_in, counts_in, ids, counts, sem):
    copies = [
        pltpu.make_async_copy(ids_in, ids, sem.at[0]),
        pltpu.make_async_copy(counts_in, counts, sem.at[1]),
    ]
    for c in copies:
        c.start()
    return copies


def list_scratch(ids, counts):
    return [pltpu.SMEM(ids.shape, ids.dtype), pltpu.SMEM(counts.shape, counts.dtype), pltpu.SemaphoreType.DMA((2,))]


def count_of(info, plane):
    return info[1][plane]


def place(info, plane, slot):
    ident = info[0][plane, slot]
    start = pl.multiple_of((2 - ident // 3) * LX, LX)
    return start, jnp.where(slot < count_of(info, plane), ident % 3, 3)


def by_count(info, plane, slots, body):
    for k in range(1, slots + 1):
        pl.when(count_of(info, plane) == k)(functools.partial(body, k))


def project_slab(info, plane, x, kp, acc):
    rows, vox = x.shape

    def body(used):
        out = dot_t(x[...], kp[plane, 0:used].reshape(used * PADW, vox))
        for s in range(used):
            row, dx = place(info, plane, s)
            acc[dx, pl.ds(row, rows), :] += out[:, s * PADW : (s + 1) * PADW]

    by_count(info, plane, kp.shape[1], body)


def back_slab(info, plane, ratios, kp, lens, finish):
    vox = kp.shape[3]

    def body(used):
        left = []
        for s in range(used):
            row, dx = place(info, plane, s)
            left.append(ratios[dx, pl.ds(row, lens), :])
        finish(dot(jnp.concatenate(left, axis=1), kp[plane, 0:used].reshape(used * PADW, vox)))

    by_count(info, plane, kp.shape[1], body)


def each_plane(planes, body):
    lax.fori_loop(0, planes, lambda z, carry: (body(z), carry)[1], 0)


def column_of(rows, width):
    return lax.rem(lax.broadcasted_iota(jnp.int32, (rows, width), 0), LX)


def fold_dx(acc):
    rows = acc.shape[1]
    col = column_of(rows, PADW)
    left = jnp.where(col > 0, pltpu.roll(acc[0], 1, 0), 0.0)
    right = jnp.where(col < LX - 1, pltpu.roll(acc[2], rows - 1, 0), 0.0)
    return acc[1] + left + right


def split_kernel(psf, after, kp):
    slots, pix, planes, vox = psf.shape
    full = pix // 16 * 16
    kp[:, :, full:PADW, :] = jnp.zeros((planes, slots, PADW - full, vox), BF)
    for s in range(slots):
        both = jnp.swapaxes(psf[s], 0, 1)
        for z in range(planes):
            kp[z, s, 0:pix, :] = both[z]


def split_call(psf, after):
    planes, slots, pix, vox = psf.shape
    return pl.pallas_call(
        split_kernel,
        out_shape=jax.ShapeDtypeStruct((planes, slots, PADW, vox), BF),
        in_specs=[VMEM, ANY],
        out_specs=VMEM,
        compiler_params=pltpu.CompilerParams(vmem_limit_bytes=SPLIT_VMEM),
        cost_estimate=cost(5),
        name="split_planes",
    )(jnp.transpose(psf, (1, 2, 0, 3)), after)


def first_kernel(ids_in, counts_in, est, kp, part_out, send_out, est_out, xs, acc, ids, counts, sem):
    copies = fetch(ids_in, counts_in, ids, counts, sem)
    acc[0:3] = jnp.zeros((3,) + acc.shape[1:], F32)

    def body(z):
        t = est[z].T
        est_out[z] = t
        xs[...] = t.astype(BF)
        project_slab((ids, counts), z, xs, kp, acc)

    for c in copies:
        c.wait()
    each_plane(est.shape[0], body)
    keep_part(fold_dx(acc), part_out, send_out)


def first_call(estimate, kp, ids, counts):
    planes, vox, lens = estimate.shape
    rows = lens + 2 * LX
    return pl.pallas_call(
        first_kernel,
        out_shape=(
            jax.ShapeDtypeStruct((rows, PADW), F32),
            jax.ShapeDtypeStruct((2 * LX, PADW), BF),
            jax.ShapeDtypeStruct((planes, lens, vox), F32),
        ),
        in_specs=[ANY, ANY, VMEM, VMEM],
        out_specs=(VMEM, VMEM, VMEM),
        scratch_shapes=[
            pltpu.VMEM((lens, vox), BF),
            pltpu.VMEM((4, rows, PADW), F32),
        ]
        + list_scratch(ids, counts),
        compiler_params=pltpu.CompilerParams(vmem_limit_bytes=36 << 20),
        cost_estimate=cost(5),
        name="project_first",
    )(ids, counts, estimate, kp)


def cost(us):
    return pl.CostEstimate(flops=int(us * 1e9), bytes_accessed=int(us * 3e6), transcendentals=0)


def upward():
    return lax.rem(lax.axis_index("band") + lax.axis_index("depth"), 2) == 1


def sensor_kernel(meas, bg, out, edge):
    pix, lens = meas.shape
    out[...] = jnp.zeros(out.shape, F32)
    out[0, :, 0:pix] = meas[...].T
    out[1, :, 0:pix] = bg[...].T
    line = pl.multiple_of(jnp.where(upward(), lens - LX, 0), LX)
    edge[:, 0:LX] = out[:, pl.ds(line, LX), :]
    edge[:, LX:] = jnp.zeros((2, edge.shape[1] - LX, PADW), F32)


def sensor_call(measured, background):
    lens = measured.shape[1]
    return pl.pallas_call(
        sensor_kernel,
        out_shape=(
            jax.ShapeDtypeStruct((2, lens, PADW), F32),
            jax.ShapeDtypeStruct((2, LX + 8, PADW), F32),
        ),
        in_specs=[VMEM, VMEM],
        out_specs=(VMEM, VMEM),
        compiler_params=pltpu.CompilerParams(vmem_limit_bytes=16 << 20),
        cost_estimate=cost(8),
        name="sensor_turn",
    )(measured, background)


def keep_part(total, part_out, send_out):
    part_out[...] = total
    rows = part_out.shape[0]
    start = pl.multiple_of(jnp.where(upward(), 0, rows - 2 * LX), LX)
    send_out[...] = part_out[pl.ds(start, 2 * LX), :].astype(BF)


def edge_kernel(own, other, out):
    rows = own.shape[0]
    up = upward()
    base = pl.multiple_of(jnp.where(up, rows - 2 * LX, 0), LX)
    for i in range(2):
        line = pl.multiple_of(jnp.where(up, LX - i * LX, i * LX), LX)
        out[i] = (own[pl.ds(base + line, LX), :] + other[pl.ds(line, LX), :].astype(F32)).astype(BF)


def edge_call(own, other):
    return pl.pallas_call(
        edge_kernel,
        out_shape=jax.ShapeDtypeStruct((2, LX, PADW), BF),
        in_specs=[VMEM, VMEM],
        out_specs=VMEM,
        compiler_params=pltpu.CompilerParams(vmem_limit_bytes=16 << 20),
        cost_estimate=cost(0.3),
        name="edge_rows",
    )(own, other)


def ratio_rows(own, other, start, size, extra, measured, background, keep):
    total = own[start : start + size, :] + other[start : start + size, :]
    if extra is not None:
        total = total + extra
    return jnp.where(keep, measured / (total + background), 0.0).astype(BF).astype(F32)


def spread(planes_ref, start, whole):
    rows = whole.shape[0]
    col = column_of(rows, PADW)
    here = pl.ds(start, rows)
    planes_ref[1, here, :] = whole.astype(BF)
    planes_ref[2, here, :] = jnp.where(col > 0, pltpu.roll(whole, 1, 0), 0.0).astype(BF)
    planes_ref[0, here, :] = jnp.where(col < LX - 1, pltpu.roll(whole, rows - 1, 0), 0.0).astype(BF)


def real_lanes(pix):
    return lax.broadcasted_iota(jnp.int32, (1, PADW), 1) < pix


def inner_kernel(pix, own, other, sensor, out):
    size = out.shape[1]
    measured, background = (sensor[i, LX : LX + size] for i in range(2))
    spread(out, 0, ratio_rows(own, other, 2 * LX, size, None, measured, background, real_lanes(pix)))


def inner_call(pix, own, other, sensor):
    return pl.pallas_call(
        functools.partial(inner_kernel, pix),
        out_shape=jax.ShapeDtypeStruct((3, own.shape[0] - 4 * LX, PADW), BF),
        in_specs=[VMEM] * 3,
        out_specs=VMEM,
        compiler_params=pltpu.CompilerParams(vmem_limit_bytes=16 << 20),
        cost_estimate=cost(1),
        name="inner_ratio",
    )(own, other, sensor)


def ratio_planes(own, other, mine, theirs, inner, sensor, sensor_mine, sensor_theirs, planes_ref, pix):
    rows = own.shape[0]
    lens = rows - 2 * LX
    band = lax.axis_index("band")
    up = upward()

    def both(a, b):
        pair = [(a[i, 0:LX].astype(F32), b[i, 0:LX].astype(F32)) for i in range(2)]
        return [jnp.where(up, x, y) for x, y in pair], [jnp.where(up, y, x) for x, y in pair]

    upper, lower = both(mine, theirs)
    sensor_up, sensor_low = both(sensor_mine, sensor_theirs)
    below = band > 0
    above = band < lax.axis_size("band") - 1
    lane = real_lanes(pix)

    def ratio(start, extra, measured, background, keep):
        return ratio_rows(own, other, start, LX, extra, measured, background, keep)

    planes_ref[0:3, 2 * LX : lens, :] = inner[...]
    planes_ref[3] = jnp.zeros((rows, PADW), BF)
    low = [
        ratio(0, lower[1], sensor_low[0], sensor_low[1], lane & below),
        ratio(LX, jnp.where(below, lower[0], 0.0), sensor[0, 0:LX], sensor[1, 0:LX], lane),
    ]
    spread(planes_ref, 0, jnp.concatenate(low, axis=0))
    high = [
        ratio(lens, jnp.where(above, upper[0], 0.0), sensor[0, lens - LX :], sensor[1, lens - LX :], lane),
        ratio(lens + LX, upper[1], sensor_up[0], sensor_up[1], lane & above),
    ]
    spread(planes_ref, lens, jnp.concatenate(high, axis=0))


def sensitivity_kernel(ids, counts, kp, after, inv_out):
    planes, even, _, vox = kp.shape
    lens = inv_out.shape[1]
    width = even * PADW
    lane = lax.broadcasted_iota(jnp.int32, (16, width), 1)
    slot = lax.broadcasted_iota(jnp.int32, (16, width), 0)
    ones = jnp.where(lane // PADW == slot, 1.0, 0.0).astype(BF)
    lane = lax.broadcasted_iota(jnp.int32, (1, 128), 1)
    slot = lax.rem(lane, 16)
    l = lax.broadcasted_iota(jnp.int32, (lens, 128), 0)
    grid_rows = lens // LX * lax.axis_size("band")
    row = lax.axis_index("band") * (lens // LX) + l // LX
    col = lax.rem(l, LX)

    def body(z):
        sums = dot(ones, kp[z].reshape(width, vox))
        high = sums.astype(BF).astype(F32)
        mid = (sums - high).astype(BF).astype(F32)
        low = sums - high - mid
        right = jnp.concatenate([high, mid, low, jnp.zeros((80, vox), F32)], axis=0).astype(BF)
        dy = jnp.zeros((1, 128), jnp.int32)
        dx = jnp.zeros((1, 128), jnp.int32)
        for s in range(ids.shape[1]):
            dy = jnp.where(slot == s, ids[z, s] // 3 - 1, dy)
            dx = jnp.where(slot == s, ids[z, s] % 3 - 1, dx)
        active = (slot < counts[z]) & (lane < 48)
        r = row - dy
        c = col - dx
        inside = (r >= 0) & (r < grid_rows) & (c >= 0) & (c < LX) & active
        inv_out[z] = 1.0 / dot(jnp.where(inside, 1.0, 0.0).astype(BF), right)

    each_plane(planes, body)


def sensitivity_call(ids, counts, kp, lens, after):
    planes, _, _, vox = kp.shape
    return pl.pallas_call(
        sensitivity_kernel,
        out_shape=jax.ShapeDtypeStruct((planes, lens, vox), F32),
        in_specs=[SMEM, SMEM, VMEM, ANY],
        out_specs=VMEM,
        compiler_params=pltpu.CompilerParams(vmem_limit_bytes=16 << 20),
        cost_estimate=cost(3),
        name="sensitivity",
    )(ids, counts, kp, after)


def middle_kernel(
    pix, ids_in, counts_in, own, other, mine, theirs, inner, sensor, sensor_mine, sensor_theirs, est, inv, kp,
    part_out, send_out, vol_out, ratios, xs, acc, ids, counts, sem,
):
    copies = fetch(ids_in, counts_in, ids, counts, sem)
    ratio_planes(own, other, mine, theirs, inner, sensor, sensor_mine, sensor_theirs, ratios, pix)
    acc[0:3] = jnp.zeros((3,) + acc.shape[1:], F32)

    def body(z):
        def finish(back):
            vol = est[z] * back * inv[z]
            vol_out[z] = vol
            xs[...] = vol.astype(BF)

        back_slab((ids, counts), z, ratios, kp, est.shape[1], finish)
        project_slab((ids, counts), z, xs, kp, acc)

    for c in copies:
        c.wait()
    each_plane(est.shape[0], body)
    keep_part(fold_dx(acc), part_out, send_out)


def middle_call(pix, ids, counts, own, other, mine, theirs, inner, sensors, est, inv, kp):
    planes, lens, vox = est.shape
    rows = own.shape[0]
    return pl.pallas_call(
        functools.partial(middle_kernel, pix),
        out_shape=(
            jax.ShapeDtypeStruct((rows, PADW), F32),
            jax.ShapeDtypeStruct((2 * LX, PADW), BF),
            jax.ShapeDtypeStruct((planes, lens, vox), F32),
        ),
        in_specs=[ANY, ANY] + [VMEM] * 11,
        out_specs=(VMEM,) * 3,
        scratch_shapes=[
            pltpu.VMEM((4, rows, PADW), BF),
            pltpu.VMEM((lens, vox), BF),
            pltpu.VMEM((4, rows, PADW), F32),
        ]
        + list_scratch(ids, counts),
        compiler_params=pltpu.CompilerParams(vmem_limit_bytes=36 << 20),
        cost_estimate=cost(10),
        name="back_and_project",
    )(ids, counts, own, other, mine, theirs, inner, *sensors, est, inv, kp)


def last_kernel(
    pix, ids_in, counts_in, own, other, mine, theirs, inner, sensor, sensor_mine, sensor_theirs, vol, inv, kp,
    out, ratios, turned, sem, ids, counts, list_sem,
):
    copies = fetch(ids_in, counts_in, ids, counts, list_sem)
    ratio_planes(own, other, mine, theirs, inner, sensor, sensor_mine, sensor_theirs, ratios, pix)

    vox = vol.shape[2]

    def copy(z, v):
        here = pl.ds(v * 128, 128)
        return pltpu.make_async_copy(turned.at[z, here], out.at[z, here], sem.at[z, v])

    def body(z):
        def finish(back):
            for v in range(vox // 128):
                here = slice(v * 128, (v + 1) * 128)
                turned[z, here, :] = (vol[z, :, here] * back[:, here] * inv[z, :, here]).T
                copy(z, v).start()

        back_slab((ids, counts), z, ratios, kp, vol.shape[1], finish)

    for c in copies:
        c.wait()
    each_plane(vol.shape[0], body)
    for z in range(vol.shape[0]):
        for v in range(vox // 128):
            copy(z, v).wait()


def last_call(pix, ids, counts, own, other, mine, theirs, inner, sensors, vol, inv, kp):
    planes, lens, vox = vol.shape
    rows = own.shape[0]
    return pl.pallas_call(
        functools.partial(last_kernel, pix),
        out_shape=jax.ShapeDtypeStruct((planes, vox, lens), F32),
        in_specs=[ANY, ANY] + [VMEM] * 11,
        out_specs=ANY,
        scratch_shapes=[
            pltpu.VMEM((4, rows, PADW), BF),
            pltpu.VMEM((planes, vox, lens), F32),
            pltpu.SemaphoreType.DMA((planes, vox // 128)),
        ]
        + list_scratch(ids, counts),
        compiler_params=pltpu.CompilerParams(vmem_limit_bytes=36 << 20),
        cost_estimate=cost(6),
        name="back_last",
    )(ids, counts, own, other, mine, theirs, inner, *sensors, vol, inv, kp)


def swap(x):
    return lax.ppermute(x, "depth", [(0, 1), (1, 0)])


def edge_exchange(x):
    parts, bands, depth = (lax.axis_size(a) for a in ("parts", "band", "depth"))
    pairs = []
    for p in range(parts):
        for b in range(bands):
            for d in range(depth):
                q, c = p, b + (1 if (b + d) % 2 == 1 else -1)
                if c < 0 or c == bands:
                    q, c = min(p ^ 1, parts - 1), b
                pairs.append(((p * bands + b) * depth + d, (q * bands + c) * depth + d))
    return lax.ppermute(x, ("parts", "band", "depth"), pairs)


def per_device(estimate, psf_blocks, offset_ids, block_counts, measured, background):
    pix, lens = measured.shape
    sensor, sensor_edge = sensor_call(measured, background)
    sensor_mine = edge_exchange(sensor_edge)
    kp = split_call(psf_blocks, sensor_edge)
    part, send, est = first_call(estimate, kp, offset_ids, block_counts)
    sum_edge, sensor_mine = lax.optimization_barrier((swap(send), sensor_mine))
    edges, part = lax.optimization_barrier((edge_call(part, sum_edge), part))
    mine = edge_exchange(edges)
    inv = sensitivity_call(offset_ids, block_counts, kp, lens, edges)
    other = swap(part)
    sensors = (sensor, sensor_mine, swap(sensor_mine))
    inner = inner_call(pix, part, other, sensor)
    mine, inv, inner = lax.optimization_barrier((mine, inv, inner))
    part, send, vol = middle_call(
        pix, offset_ids, block_counts, part, other, mine, swap(mine), inner, sensors, est, inv, kp
    )
    edges, part = lax.optimization_barrier((edge_call(part, swap(send)), part))
    mine = edge_exchange(edges)
    other = swap(part)
    inner = inner_call(pix, part, other, sensor)
    mine, inner = lax.optimization_barrier((mine, inner))
    return last_call(pix, offset_ids, block_counts, part, other, mine, swap(mine), inner, sensors, vol, inv, kp)


def solution(mesh):
    in_specs = (
        P("depth", "parts", "band"),
        P("depth", None, None, None),
        P("depth", None),
        P("depth"),
        P("parts", "band"),
        P("parts", "band"),
    )
    return jax.shard_map(
        per_device, mesh=mesh, in_specs=in_specs, out_specs=P("depth", "parts", "band"), check_vma=False
    )
```
